32 devices in a mesh: section: 8 (over z, y), blk: 4 (over x, core).
Axes of the slice: x: 2, y: 2, z: 4, core: 2. Of those that a mesh axis runs over, the one named last changes fastest.
Arguments:
- pending_groups: bfloat16 [512, 16384], P('section', 'blk'), may hold values from -6 to 6
- coefficient_tiles: bfloat16 [8, 128, 8, 128, 128], P('section', 'blk'), may hold values from -0.25 to 0.25
- source_block_indices: int32 [8, 128, 8], P('section', 'blk'), may hold values from 0 to 127, as said below
- additive_offsets: float32 [8, 16384], P('section', 'blk'), may hold values from -1.75 to 1.75
Outputs:
- emitted: bfloat16 [8, 512, 16384], P(None, 'section', 'blk')
The draws below stay inside these ranges and needn't reach their ends.
Inputs may be any that keep to these rules, and one draw needn't show every extreme that they name: `source_block_indices`: within a block-row the 8 block columns are distinct. A block-row held by index d of blk (block-rows d*32 to (d+1)*32 - 1) uses only block columns d*32 - 4 to (d+1)*32 + 3, taken modulo 128; in every layer the first block-row of each index uses column d*32 - 4 and the last uses (d+1)*32 + 3.
All inputs are finite; a program needn't handle non-finite values.
Results may differ from the reference program's by a relative error of at most 0.013.
Values may be sent and summed in bfloat16 or wider, within the bound.
No kernel may reach another device: no remote copies, remote signals or barrier semaphores. Data moves between devices by JAX's collectives and lax.ppermute only.
A program may use at most 64 MiB of HBM per device.

```python
import jax
import jax.numpy as jnp
from jax import lax

BLK = 128
BR_DEV = 32
NZB = 8
HALO = 4
GROUP_HEIGHT = 64
TICKS = 8
DEPTH_OF_NET = 8
NB = 128
UNITS_PER_LEVEL = 16384


def draw_source_block_indices(key, part):
    window = BR_DEV + 2 * HALO
    scores = jax.random.randint(key, (DEPTH_OF_NET, NB, window), 0, 1 << 20)
    offsets = jnp.arange(window, dtype=jnp.int32)
    local_row = jnp.arange(NB, dtype=jnp.int32) % BR_DEV
    ranked = scores * window + offsets[None, None, :]
    first_edge = (local_row[:, None] == 0) & (offsets[None, :] == 0)
    last_edge = (local_row[:, None] == BR_DEV - 1) & (offsets[None, :] == window - 1)
    ranked = jnp.where((first_edge | last_edge)[None, :, :], -1, ranked)
    chosen = jnp.argsort(ranked, axis=-1)[:, :, :NZB].astype(jnp.int32)
    owner_start = jnp.arange(NB, dtype=jnp.int32) // BR_DEV * BR_DEV
    return jnp.mod(owner_start[None, :, None] - HALO + chosen, NB).astype(jnp.int32)


def level_of(stream_key, shape, cuts, least, top_value):
    factor_of, own = 1.0, jax.random.fold_in(stream_key, 6)
    for dim, blocks in cuts:
        steps = jnp.exp(jax.random.uniform(jax.random.fold_in(own, dim), (blocks,), jnp.float32, least / len(cuts), top_value / len(cuts)))
        factor_of = factor_of * jnp.repeat(steps, shape[dim] // blocks).reshape([-1 if axis == dim else 1 for axis in range(len(shape))])
    return factor_of


def centred(key, extent, spread, reach, shards=(), held_as=jnp.bfloat16):
    array = jax.random.normal(key, extent, jnp.float32) * spread
    if len(shards) > 0:
        array = level_of(key, extent, shards, -0.22, 0.18) * array
    return jnp.clip(array, min=-reach, max=reach).astype(held_as)


def setup_inputs(seed: int = 0) -> dict:
    splits = jax.random.split(jax.random.key(seed), 5)
    return {
        "pending_groups": centred(splits[0], (DEPTH_OF_NET * GROUP_HEIGHT, UNITS_PER_LEVEL), 1.0, 6.0, ((0, 8), (1, 4))),
        "coefficient_tiles": centred(splits[1], (DEPTH_OF_NET, NB, NZB, BLK, BLK), (NZB * BLK // 2) ** -0.5, 0.25, ((0, 8), (1, 4))),
        "source_block_indices": draw_source_block_indices(jax.random.fold_in(splits[4], 71), 0),
        "additive_offsets": centred(splits[3], (DEPTH_OF_NET, UNITS_PER_LEVEL), 0.3, 1.75, ((0, 8), (1, 4)), jnp.float32),
    }


def layer_apply(forwarded_activations, layer_weights, layer_cols, layer_bias):
    row_count = forwarded_activations.shape[0]
    blocks = forwarded_activations.reshape(row_count, NB, BLK).astype(jnp.float32)
    picked = blocks[:, layer_cols]
    summed = jnp.einsum("mikc,ikcd->mid", picked, layer_weights.astype(jnp.float32))
    summed = summed.reshape(row_count, NB * BLK) + layer_bias
    return jnp.maximum(summed, 0.0)


def one_layer(operands):
    return layer_apply(operands[0], operands[1], operands[2], operands[3])


def reference(pending_groups, coefficient_tiles, source_block_indices, additive_offsets):
    forwarded_activations = pending_groups.reshape(DEPTH_OF_NET, GROUP_HEIGHT, UNITS_PER_LEVEL)
    emitted = []
    for tick_index in range(TICKS):
        produced = lax.map(one_layer, (forwarded_activations, coefficient_tiles, source_block_indices, additive_offsets))
        live_mask = (jnp.arange(DEPTH_OF_NET) >= tick_index)[:, None, None]
        produced = jnp.where(live_mask, produced, 0.0).astype(jnp.bfloat16)
        emitted.append(produced.reshape(DEPTH_OF_NET * GROUP_HEIGHT, UNITS_PER_LEVEL))
        forwarded_activations = jnp.concatenate([jnp.zeros((1, GROUP_HEIGHT, UNITS_PER_LEVEL), jnp.bfloat16), produced[:-1]], axis=0)
    return jnp.stack(emitted)
```

```python
import functools

import jax
import jax.numpy as jnp
from jax import lax
from jax.experimental import pallas as pl
from jax.experimental.pallas import tpu as pltpu
from jax.sharding import PartitionSpec as P

BLK = 128
HALO = 4
TICKS = 8
CHUNKS = 2


def layer_kernel(tick, src_row, dst_row, rows, brs, nzb, meta, main, low, high, w, bias, emitted_in, emitted, out, left, right, xbuf, sem):
    del emitted_in
    edge = HALO * BLK
    width = brs * BLK
    live = meta[brs * nzb] >= tick

    @pl.when(live)
    def _():
        src = pl.ds(src_row, rows)
        xbuf[:, 0:edge] = low[src, :]
        xbuf[:, edge : edge + width] = main[src, :]
        xbuf[:, edge + width : edge + width + edge] = high[src, :]
        for i in range(brs):
            picked = jnp.concatenate(
                [
                    xbuf[:, pl.ds(pl.multiple_of(meta[i * nzb + k] * BLK, BLK), BLK)]
                    for k in range(nzb)
                ],
                axis=1,
            )
            cols = pl.ds(i * BLK, BLK)
            summed = jnp.dot(picked, w[i], preferred_element_type=jnp.float32) + bias[:, cols]
            made = jnp.maximum(summed, 0.0).astype(jnp.bfloat16)
            out[:, cols] = made
            if i < HALO:
                left[:, cols] = made
            if i >= brs - HALO:
                right[:, pl.ds((i - brs + HALO) * BLK, BLK)] = made

    @pl.when(jnp.logical_not(live))
    def _():
        out[...] = jnp.zeros_like(out)
        left[...] = jnp.zeros_like(left)
        right[...] = jnp.zeros_like(right)

    copy = pltpu.make_async_copy(out, emitted.at[tick, pl.ds(dst_row, rows), :], sem)
    copy.start()
    copy.wait()


def apply_layer(tick, src_row, dst_row, rows, meta, main, low, high, w, bias, emitted, out_aval):
    brs = w.shape[0]
    nzb = w.shape[1] // BLK
    width = brs * BLK
    edge = HALO * BLK
    vmem = pl.BlockSpec(memory_space=pltpu.VMEM)
    anywhere = pl.BlockSpec(memory_space=pl.ANY)
    body = functools.partial(layer_kernel, tick, src_row, dst_row, rows, brs, nzb)
    operands = [
        pltpu.with_memory_space_constraint(meta, pltpu.SMEM),
        main,
        low,
        high,
        pltpu.with_memory_space_constraint(w, pltpu.VMEM),
        bias,
    ]
    specs = [pl.BlockSpec(memory_space=pltpu.SMEM), vmem, vmem, vmem, vmem, vmem]
    aliases = {}
    if emitted is not None:
        operands.append(emitted)
        specs.append(anywhere)
        aliases = {6: 0}
    else:
        inner = body
        body = lambda *refs: inner(*refs[:6], None, *refs[6:])
    return pl.pallas_call(
        body,
        out_shape=(
            out_aval,
            jax.ShapeDtypeStruct((rows, width), jnp.bfloat16),
            jax.ShapeDtypeStruct((rows, edge), jnp.bfloat16),
            jax.ShapeDtypeStruct((rows, edge), jnp.bfloat16),
        ),
        in_specs=specs,
        out_specs=(anywhere, vmem, vmem, vmem),
        scratch_shapes=[
            pltpu.VMEM((rows, width + 2 * edge), jnp.bfloat16),
            pltpu.SemaphoreType.DMA,
        ],
        input_output_aliases=aliases,
        compiler_params=pltpu.CompilerParams(vmem_limit_bytes=8 * 1024 * 1024),
        cost_estimate=pl.CostEstimate(
            flops=2 * rows * brs * nzb * BLK * BLK, bytes_accessed=w.size * 2, transcendentals=0
        ),
        name=f"layer_t{tick}_r{dst_row}",
    )(*operands)


def shards(sections, blks, pending_groups, coefficient_tiles, source_block_indices, additive_offsets):
    block_rows, nzb = coefficient_tiles.shape[1:3]
    height, width = pending_groups.shape
    rows = height // CHUNKS
    edge = HALO * BLK
    section = lax.axis_index("section")
    me = lax.axis_index("blk")
    local_cols = jnp.mod(source_block_indices[0] - me * block_rows + HALO, block_rows * blks)
    meta = jnp.concatenate([local_cols.reshape(-1), section.astype(jnp.int32)[None]])
    w = coefficient_tiles.reshape(block_rows, nzb * BLK, BLK)
    emitted_aval = jax.ShapeDtypeStruct((TICKS, height, width), jnp.bfloat16)

    def ring(shift):
        return [(i, (i + shift) % blks) for i in range(blks)]

    def onward(first, shift):
        return [
            (s * blks + i, (s + 1) * blks + (i + shift) % blks)
            for s in range(first, sections - 1)
            for i in range(blks)
        ]

    low = lax.ppermute(pending_groups[:, width - edge :], "blk", ring(1))
    high = lax.ppermute(pending_groups[:, :edge], "blk", ring(-1))
    parts = [(pending_groups, low, high, c * rows) for c in range(CHUNKS)]
    emitted = None
    for tick in range(TICKS):
        for c in range(CHUNKS):
            main, low, high, src_row = parts[c]
            emitted, out, left, right = apply_layer(
                tick, src_row, c * rows, rows, meta, main, low, high, w, additive_offsets, emitted, emitted_aval
            )
            if tick + 1 < TICKS:
                axes = ("section", "blk")
                parts[c] = (
                    lax.ppermute(out, axes, onward(tick, 0)),
                    lax.ppermute(right, axes, onward(tick, 1)),
                    lax.ppermute(left, axes, onward(tick, -1)),
                    0,
                )
    return emitted


def solution(mesh):
    in_specs = (
        P("section", "blk"),
        P("section", "blk", None, None, None),
        P("section", "blk", None),
        P("section", "blk"),
    )
    out_specs = P(None, "section", "blk")
    body = functools.partial(shards, mesh.shape["section"], mesh.shape["blk"])
    return jax.shard_map(body, mesh=mesh, in_specs=in_specs, out_specs=out_specs, check_vma=False)
```

```python
import functools

import jax
import jax.numpy as jnp
from jax import lax
from jax.experimental import pallas as pl
from jax.experimental.pallas import tpu as pltpu
from jax.sharding import PartitionSpec as P

BLK = 128
HALO = 4
TICKS = 8
CHUNKS = 2
VMEM = pl.BlockSpec(memory_space=pltpu.VMEM)
SMEM = pl.BlockSpec(memory_space=pltpu.SMEM)
ANY = pl.BlockSpec(memory_space=pl.ANY)


def load_kernel(state, w, bias, state_out, w_out, bias_out, sems):
    copies = [
        pltpu.make_async_copy(src, dst, sems.at[i])
        for i, (src, dst) in enumerate(((state, state_out), (bias, bias_out), (w, w_out)))
    ]
    for copy in copies:
        copy.start()
    for copy in copies:
        copy.wait()


def load(*arrays):
    return pl.pallas_call(
        load_kernel,
        out_shape=tuple(pltpu.VMEM(a.shape, a.dtype) for a in arrays),
        in_specs=[ANY] * 3,
        out_specs=(VMEM,) * 3,
        scratch_shapes=[pltpu.SemaphoreType.DMA((3,))],
        compiler_params=pltpu.CompilerParams(vmem_limit_bytes=16 * 1024 * 1024),
        cost_estimate=pl.CostEstimate(flops=0, bytes_accessed=arrays[1].size * 2, transcendentals=0),
        name="load",
    )(*(pltpu.with_memory_space_constraint(a, pltpu.HBM) for a in arrays))


def layer_kernel(tick, src_row, rows, brs, nzb, own_slot, prev_slot, aliased, *refs):
    refs = list(refs)
    meta, main, low, high, w, bias = refs[:6]
    del refs[:6]
    prev = refs.pop(0) if prev_slot is not None else None
    if aliased:
        refs.pop(0)
    emitted = refs.pop(0) if prev_slot is not None or own_slot is not None else None
    out, xbuf, sems = refs
    edge = HALO * BLK
    width = brs * BLK

    def write(src, slot, sem):
        slot_tick, row = slot
        return pltpu.make_async_copy(src, emitted.at[slot_tick, pl.ds(row, rows), :], sem)

    if prev is not None:
        write(prev, prev_slot, sems.at[0]).start()
    live = meta[brs * nzb] >= tick

    @pl.when(live)
    def _():
        src = pl.ds(src_row, rows)
        xbuf[:, 0:edge] = low[src, :]
        xbuf[:, edge : edge + width] = main[src, :]
        xbuf[:, edge + width : edge + width + edge] = high[src, :]
        for i in range(brs):
            picked = jnp.concatenate(
                [
                    xbuf[:, pl.ds(pl.multiple_of(meta[i * nzb + k] * BLK, BLK), BLK)]
                    for k in range(nzb)
                ],
                axis=1,
            )
            cols = pl.ds(i * BLK, BLK)
            summed = jnp.dot(picked, w[i], preferred_element_type=jnp.float32) + bias[:, cols]
            out[:, cols] = jnp.maximum(summed, 0.0).astype(jnp.bfloat16)

    @pl.when(jnp.logical_not(live))
    def _():
        out[...] = jnp.zeros_like(out)

    if own_slot is not None:
        write(out, own_slot, sems.at[1]).start()
    if prev is not None:
        write(prev, prev_slot, sems.at[0]).wait()
    if own_slot is not None:
        write(out, own_slot, sems.at[1]).wait()


def apply_layer(tick, src_row, row, rows, last, operands, prev, prev_slot, emitted, emitted_aval):
    meta, main, low, high, w, bias = operands
    brs, depth = w.shape[:2]
    nzb = depth // BLK
    width = brs * BLK
    edge = HALO * BLK
    args = [
        pltpu.with_memory_space_constraint(meta, pltpu.SMEM),
        *(pltpu.with_memory_space_constraint(a, pltpu.VMEM) for a in (main, low, high, w, bias)),
    ]
    specs = [SMEM] + [VMEM] * 5
    out_shape = []
    out_specs = []
    scratch = [
        pltpu.VMEM((rows, width + 2 * edge), jnp.bfloat16),
        pltpu.SemaphoreType.DMA((2,)),
    ]
    aliases = {}
    if prev is not None:
        args.append(pltpu.with_memory_space_constraint(prev, pltpu.VMEM))
        specs.append(VMEM)
    if emitted is not None:
        aliases = {len(args): 0}
        args.append(emitted)
        specs.append(ANY)
    if prev is not None or last:
        out_shape.append(emitted_aval)
        out_specs.append(ANY)
    if last:
        scratch.insert(0, pltpu.VMEM((rows, width), jnp.bfloat16))
    else:
        out_shape.append(pltpu.VMEM((rows, width), jnp.bfloat16))
        out_specs.append(VMEM)
    body = functools.partial(
        layer_kernel, tick, src_row, rows, brs, nzb, (tick, row) if last else None, prev_slot, emitted is not None
    )
    return pl.pallas_call(
        body,
        out_shape=tuple(out_shape),
        in_specs=specs,
        out_specs=tuple(out_specs),
        scratch_shapes=scratch,
        input_output_aliases=aliases,
        compiler_params=pltpu.CompilerParams(vmem_limit_bytes=8 * 1024 * 1024),
        cost_estimate=pl.CostEstimate(
            flops=2 * rows * brs * nzb * BLK * BLK, bytes_accessed=w.size * 2, transcendentals=0
        ),
        name=f"layer_t{tick}_r{row}",
    )(*args)


def edges_kernel(main, after, left, right):
    del after
    edge = HALO * BLK
    left[...] = main[:, 0:edge]
    right[...] = main[:, main.shape[1] - edge :]


def edges(main, after):
    aval = pltpu.VMEM((main.shape[0], HALO * BLK), main.dtype)
    return pl.pallas_call(
        edges_kernel,
        out_shape=(aval, aval),
        in_specs=[VMEM, ANY],
        out_specs=(VMEM, VMEM),
        name="edges",
    )(pltpu.with_memory_space_constraint(main, pltpu.VMEM), after)


def shards(sections, blks, pending_groups, coefficient_tiles, source_block_indices, additive_offsets):
    block_rows, nzb = coefficient_tiles.shape[1:3]
    height, width = pending_groups.shape
    rows = height // CHUNKS
    edge = HALO * BLK
    section = lax.axis_index("section")
    me = lax.axis_index("blk")
    emitted_aval = jax.ShapeDtypeStruct((TICKS, height, width), jnp.bfloat16)

    def cycle(axis, count, shift, values):
        return lax.ppermute(values, axis, [(i, (i + shift) % count) for i in range(count)])

    def halos(left, right):
        return cycle("blk", blks, 1, right), cycle("blk", blks, -1, left)

    low, high = halos(pending_groups[:, :edge], pending_groups[:, width - edge :])
    state, w, bias = load(
        pending_groups, coefficient_tiles.reshape(block_rows, nzb * BLK, BLK), additive_offsets
    )
    local_cols = jnp.mod(source_block_indices[0] - me * block_rows + HALO, block_rows * blks)
    meta = jnp.concatenate([local_cols.reshape(-1), section.astype(jnp.int32)[None]])
    parts = [state] * CHUNKS
    emitted = prev = prev_slot = None
    for tick in range(TICKS):
        last = tick + 1 == TICKS
        for c in range(CHUNKS):
            src_row = c * rows
            if tick > 0:
                low, high = halos(*edges(parts[c], made))
                src_row = 0
            outs = list(
                apply_layer(
                    tick, src_row, c * rows, rows, last, (meta, parts[c], low, high, w, bias), prev, prev_slot, emitted, emitted_aval
                )
            )
            if prev is not None or last:
                emitted = outs.pop(0)
            prev = prev_slot = None
            made = emitted if last else outs[0]
            if not last:
                prev, prev_slot = outs[0], (tick, c * rows)
                parts[c] = cycle("section", sections, 1, prev)
    return emitted


def solution(mesh):
    in_specs = (
        P("section", "blk"),
        P("section", "blk", None, None, None),
        P("section", "blk", None),
        P("section", "blk"),
    )
    out_specs = P(None, "section", "blk")
    body = functools.partial(shards, mesh.shape["section"], mesh.shape["blk"])
    return jax.shard_map(body, mesh=mesh, in_specs=in_specs, out_specs=out_specs, check_vma=False)
```

```python
import functools

import jax
import jax.numpy as jnp
from jax import lax
from jax.experimental import pallas as pl
from jax.experimental.pallas import tpu as pltpu
from jax.sharding import PartitionSpec as P

BLK = 128
HALO = 4
TICKS = 8
CHUNKS = 2
VMEM = pl.BlockSpec(memory_space=pltpu.VMEM)
SMEM = pl.BlockSpec(memory_space=pltpu.SMEM)
ANY = pl.BlockSpec(memory_space=pl.ANY)


def load_kernel(state, w, bias, state_out, w_out, bias_out, sems):
    copies = [
        pltpu.make_async_copy(src, dst, sems.at[i])
        for i, (src, dst) in enumerate(((state, state_out), (bias, bias_out), (w, w_out)))
    ]
    for copy in copies:
        copy.start()
    for copy in copies:
        copy.wait()


def load(*arrays):
    return pl.pallas_call(
        load_kernel,
        out_shape=tuple(pltpu.VMEM(a.shape, a.dtype) for a in arrays),
        in_specs=[ANY] * 3,
        out_specs=(VMEM,) * 3,
        scratch_shapes=[pltpu.SemaphoreType.DMA((3,))],
        compiler_params=pltpu.CompilerParams(vmem_limit_bytes=16 * 1024 * 1024),
        cost_estimate=pl.CostEstimate(flops=0, bytes_accessed=arrays[1].size * 2, transcendentals=0),
        name="load",
    )(*(pltpu.with_memory_space_constraint(a, pltpu.HBM) for a in arrays))


def layer_kernel(tick, src_row, rows, brs, nzb, own_slot, prev_slot, aliased, *refs):
    refs = list(refs)
    meta, main, low, high, w, bias = refs[:6]
    del refs[:6]
    prev = refs.pop(0) if prev_slot is not None else None
    if aliased:
        refs.pop(0)
    emitted = refs.pop(0) if prev_slot is not None or own_slot is not None else None
    out, xbuf, sems = refs
    edge = HALO * BLK
    width = brs * BLK

    def write(src, slot, sem):
        slot_tick, row = slot
        return pltpu.make_async_copy(src, emitted.at[slot_tick, pl.ds(row, rows), :], sem)

    if prev is not None:
        write(prev, prev_slot, sems.at[0]).start()
    live = meta[brs * nzb] >= tick

    @pl.when(live)
    def _():
        src = pl.ds(src_row, rows)
        xbuf[:, 0:edge] = low[src, :]
        xbuf[:, edge : edge + width] = main[src, :]
        xbuf[:, edge + width : edge + width + edge] = high[src, :]
        for i in range(brs):
            picked = jnp.concatenate(
                [
                    xbuf[:, pl.ds(pl.multiple_of(meta[i * nzb + k] * BLK, BLK), BLK)]
                    for k in range(nzb)
                ],
                axis=1,
            )
            cols = pl.ds(i * BLK, BLK)
            summed = jnp.dot(picked, w[i], preferred_element_type=jnp.float32) + bias[:, cols]
            out[:, cols] = jnp.maximum(summed, 0.0).astype(jnp.bfloat16)

    @pl.when(jnp.logical_not(live))
    def _():
        out[...] = jnp.zeros_like(out)

    if own_slot is not None:
        write(out, own_slot, sems.at[1]).start()
    if prev is not None:
        write(prev, prev_slot, sems.at[0]).wait()
    if own_slot is not None:
        write(out, own_slot, sems.at[1]).wait()


def apply_layer(tick, src_row, row, rows, last, operands, prev, prev_slot, emitted, emitted_aval):
    meta, main, low, high, w, bias = operands
    brs, depth = w.shape[:2]
    nzb = depth // BLK
    width = brs * BLK
    edge = HALO * BLK
    args = [
        pltpu.with_memory_space_constraint(meta, pltpu.SMEM),
        *(pltpu.with_memory_space_constraint(a, pltpu.VMEM) for a in (main, low, high, w, bias)),
    ]
    specs = [SMEM] + [VMEM] * 5
    out_shape = []
    out_specs = []
    scratch = [
        pltpu.VMEM((rows, width + 2 * edge), jnp.bfloat16),
        pltpu.SemaphoreType.DMA((2,)),
    ]
    aliases = {}
    if prev is not None:
        args.append(pltpu.with_memory_space_constraint(prev, pltpu.VMEM))
        specs.append(VMEM)
    if emitted is not None:
        aliases = {len(args): 0}
        args.append(emitted)
        specs.append(ANY)
    if prev is not None or last:
        out_shape.append(emitted_aval)
        out_specs.append(ANY)
    if last:
        scratch.insert(0, pltpu.VMEM((rows, width), jnp.bfloat16))
    else:
        out_shape.append(pltpu.VMEM((rows, width), jnp.bfloat16))
        out_specs.append(VMEM)
    body = functools.partial(
        layer_kernel, tick, src_row, rows, brs, nzb, (tick, row) if last else None, prev_slot, emitted is not None
    )
    return pl.pallas_call(
        body,
        out_shape=tuple(out_shape),
        in_specs=specs,
        out_specs=tuple(out_specs),
        scratch_shapes=scratch,
        input_output_aliases=aliases,
        compiler_params=pltpu.CompilerParams(vmem_limit_bytes=8 * 1024 * 1024),
        cost_estimate=pl.CostEstimate(
            flops=2 * rows * brs * nzb * BLK * BLK, bytes_accessed=w.size * 2, transcendentals=0
        ),
        name=f"layer_t{tick}_r{row}",
    )(*args)


def edges_kernel(main, after, left, right):
    del after
    edge = HALO * BLK
    left[...] = main[:, 0:edge]
    right[...] = main[:, main.shape[1] - edge :]


def edges(main, after):
    aval = pltpu.VMEM((main.shape[0], HALO * BLK), main.dtype)
    return pl.pallas_call(
        edges_kernel,
        out_shape=(aval, aval),
        in_specs=[VMEM, ANY],
        out_specs=(VMEM, VMEM),
        compiler_params=pltpu.CompilerParams(vmem_limit_bytes=1024 * 1024),
        name="edges",
    )(pltpu.with_memory_space_constraint(main, pltpu.VMEM), after)


def shards(sections, blks, pending_groups, coefficient_tiles, source_block_indices, additive_offsets):
    block_rows, nzb = coefficient_tiles.shape[1:3]
    height, width = pending_groups.shape
    rows = height // CHUNKS
    edge = HALO * BLK
    section = lax.axis_index("section")
    me = lax.axis_index("blk")
    emitted_aval = jax.ShapeDtypeStruct((TICKS, height, width), jnp.bfloat16)

    def cycle(axis, count, shift, values):
        return lax.ppermute(values, axis, [(i, (i + shift) % count) for i in range(count)])

    def halos(left, right):
        return cycle("blk", blks, 1, right), cycle("blk", blks, -1, left)

    low, high = halos(pending_groups[:, :edge], pending_groups[:, width - edge :])
    state, w, bias = load(
        pending_groups, coefficient_tiles.reshape(block_rows, nzb * BLK, BLK), additive_offsets
    )
    local_cols = jnp.mod(source_block_indices[0] - me * block_rows + HALO, block_rows * blks)
    meta = jnp.concatenate([local_cols.reshape(-1), section.astype(jnp.int32)[None]])
    parts = [state] * CHUNKS
    emitted = prev = prev_slot = None
    for tick in range(TICKS):
        last = tick + 1 == TICKS
        for c in range(CHUNKS):
            src_row = c * rows
            if tick > 0:
                low, high = halos(*edges(parts[c], made))
                src_row = 0
            outs = list(
                apply_layer(
                    tick, src_row, c * rows, rows, last, (meta, parts[c], low, high, w, bias), prev, prev_slot, emitted, emitted_aval
                )
            )
            if prev is not None or last:
                emitted = outs.pop(0)
            prev = prev_slot = None
            made = emitted if last else outs[0]
            if not last:
                prev, prev_slot = outs[0], (tick, c * rows)
                parts[c] = cycle("section", sections, 1, prev)
    return emitted


def solution(mesh):
    in_specs = (
        P("section", "blk"),
        P("section", "blk", None, None, None),
        P("section", "blk", None),
        P("section", "blk"),
    )
    out_specs = P(None, "section", "blk")
    body = functools.partial(shards, mesh.shape["section"], mesh.shape["blk"])
    return jax.shard_map(body, mesh=mesh, in_specs=in_specs, out_specs=out_specs, check_vma=False)
```

```python
import functools

import jax
import jax.numpy as jnp
from jax import lax
from jax.experimental import pallas as pl
from jax.experimental.pallas import tpu as pltpu
from jax.sharding import PartitionSpec as P

BLK = 128
HALO = 4
TICKS = 8
CHUNKS = 2
VMEM = pl.BlockSpec(memory_space=pltpu.VMEM)
SMEM = pl.BlockSpec(memory_space=pltpu.SMEM)
ANY = pl.BlockSpec(memory_space=pl.ANY)


def load_kernel(blks, state, w, bias, indices, state_out, w_out, bias_out, meta, raw, sems):
    copies = [
        pltpu.make_async_copy(src, dst, sems.at[i])
        for i, (src, dst) in enumerate(((indices, raw), (state, state_out), (bias, bias_out), (w, w_out)))
    ]
    for copy in copies:
        copy.start()
    brs, nzb = indices.shape
    columns = brs * blks
    start = lax.axis_index("blk") * brs - HALO
    meta[brs * nzb] = lax.axis_index("section")
    copies[0].wait()

    @pl.loop(0, brs)
    def _(i):
        for k in range(nzb):
            col = raw[i, k] - start
            col = jnp.where(col < 0, col + columns, col)
            meta[i * nzb + k] = jnp.where(col >= columns, col - columns, col) * BLK

    for copy in copies[1:]:
        copy.wait()


def load(blks, state, w, bias, indices):
    arrays = (state, w, bias)
    return pl.pallas_call(
        functools.partial(load_kernel, blks),
        out_shape=(
            *(pltpu.VMEM(a.shape, a.dtype) for a in arrays),
            pltpu.SMEM((indices.size + 1,), jnp.int32),
        ),
        in_specs=[ANY] * 4,
        out_specs=(VMEM,) * 3 + (SMEM,),
        scratch_shapes=[pltpu.SMEM(indices.shape, jnp.int32), pltpu.SemaphoreType.DMA((4,))],
        compiler_params=pltpu.CompilerParams(vmem_limit_bytes=16 * 1024 * 1024),
        cost_estimate=pl.CostEstimate(flops=0, bytes_accessed=w.size * 2, transcendentals=0),
        name="load",
    )(*(pltpu.with_memory_space_constraint(a, pltpu.HBM) for a in (*arrays, indices)))


def layer_kernel(tick, src_row, rows, brs, nzb, own_slot, prev_slot, aliased, *refs):
    refs = list(refs)
    meta, main, low, high, w, bias = refs[:6]
    del refs[:6]
    prev = refs.pop(0) if prev_slot is not None else None
    if aliased:
        refs.pop(0)
    emitted = refs.pop(0) if prev_slot is not None or own_slot is not None else None
    left = right = None
    if own_slot is None:
        out, left, right, xbuf, sems = refs
    else:
        out, xbuf, sems = refs
    edge = HALO * BLK
    width = brs * BLK

    def write(src, slot, first, count, sem):
        where = (slice(None), pl.ds(first * BLK, count * BLK))
        slot_tick, row = slot
        return pltpu.make_async_copy(
            src.at[where], emitted.at[slot_tick, pl.ds(row, rows), pl.ds(first * BLK, count * BLK)], sem
        )

    pieces = 4
    own = []
    if own_slot is not None:
        own = [write(out, own_slot, n * brs // pieces, brs // pieces, sems.at[1 + n]) for n in range(pieces)]
    if prev is not None:
        before = write(prev, prev_slot, 0, brs, sems.at[0])
        before.start()
    live = meta[brs * nzb] >= tick

    @pl.when(live)
    def _():
        src = pl.ds(src_row, rows)
        xbuf[:, 0:edge] = low[src, :]
        xbuf[:, edge : edge + width] = main[src, :]
        xbuf[:, edge + width : edge + width + edge] = high[src, :]
        for i in range(brs):
            picked = jnp.concatenate(
                [xbuf[:, pl.ds(pl.multiple_of(meta[i * nzb + k], BLK), BLK)] for k in range(nzb)], axis=1
            )
            cols = pl.ds(i * BLK, BLK)
            summed = jnp.dot(picked, w[i], preferred_element_type=jnp.float32) + bias[:, cols]
            made = jnp.maximum(summed, 0.0).astype(jnp.bfloat16)
            out[:, cols] = made
            if left is not None and i < HALO:
                left[:, cols] = made
            if right is not None and i >= brs - HALO:
                right[:, pl.ds((i - brs + HALO) * BLK, BLK)] = made
            if own and (i + 1) % (brs // pieces) == 0:
                own[i // (brs // pieces)].start()

    @pl.when(jnp.logical_not(live))
    def _():
        out[...] = jnp.zeros_like(out)
        if left is not None:
            left[...] = jnp.zeros_like(left)
            right[...] = jnp.zeros_like(right)
        for copy in own:
            copy.start()

    if prev is not None:
        before.wait()
    for copy in own:
        copy.wait()


def apply_layer(tick, src_row, row, rows, last, operands, prev, prev_slot, emitted, emitted_aval):
    meta, main, low, high, w, bias = operands
    brs, depth = w.shape[:2]
    nzb = depth // BLK
    width = brs * BLK
    edge = HALO * BLK
    args = [
        pltpu.with_memory_space_constraint(meta, pltpu.SMEM),
        *(pltpu.with_memory_space_constraint(a, pltpu.VMEM) for a in (main, low, high, w, bias)),
    ]
    specs = [SMEM] + [VMEM] * 5
    out_shape = []
    out_specs = []
    scratch = [
        pltpu.VMEM((rows, width + 2 * edge), jnp.bfloat16),
        pltpu.SemaphoreType.DMA((5,)),
    ]
    aliases = {}
    if prev is not None:
        args.append(pltpu.with_memory_space_constraint(prev, pltpu.VMEM))
        specs.append(VMEM)
    if emitted is not None:
        aliases = {len(args): 0}
        args.append(emitted)
        specs.append(ANY)
    if prev is not None or last:
        out_shape.append(emitted_aval)
        out_specs.append(ANY)
    if last:
        scratch.insert(0, pltpu.VMEM((rows, width), jnp.bfloat16))
    else:
        out_shape += [pltpu.VMEM((rows, cols), jnp.bfloat16) for cols in (width, edge, edge)]
        out_specs += [VMEM] * 3
    body = functools.partial(
        layer_kernel, tick, src_row, rows, brs, nzb, (tick, row) if last else None, prev_slot, emitted is not None
    )
    return pl.pallas_call(
        body,
        out_shape=tuple(out_shape),
        in_specs=specs,
        out_specs=tuple(out_specs),
        scratch_shapes=scratch,
        input_output_aliases=aliases,
        compiler_params=pltpu.CompilerParams(vmem_limit_bytes=8 * 1024 * 1024),
        cost_estimate=pl.CostEstimate(
            flops=20 * rows * brs * nzb * BLK * BLK, bytes_accessed=20 * w.size, transcendentals=0
        ),
        name=f"layer_t{tick}_r{row}",
    )(*args)


def shards(sections, blks, pending_groups, coefficient_tiles, source_block_indices, additive_offsets):
    block_rows, nzb = coefficient_tiles.shape[1:3]
    height, width = pending_groups.shape
    rows = height // CHUNKS
    edge = HALO * BLK
    emitted_aval = jax.ShapeDtypeStruct((TICKS, height, width), jnp.bfloat16)

    def hop(values, step, shift):
        pairs = [
            (s * blks + i, (s + step) % sections * blks + (i + shift) % blks)
            for s in range(sections)
            for i in range(blks)
        ]
        return lax.ppermute(values, ("section", "blk"), pairs)

    low = hop(pending_groups[:, width - edge :], 0, 1)
    high = hop(pending_groups[:, :edge], 0, -1)
    state, w, bias, meta = load(
        blks,
        pending_groups,
        coefficient_tiles.reshape(block_rows, nzb * BLK, BLK),
        additive_offsets,
        source_block_indices[0],
    )
    parts = [(state, low, high, c * rows) for c in range(CHUNKS)]
    emitted = prev = prev_slot = None
    for tick in range(TICKS):
        last = tick + 1 == TICKS
        for c in range(CHUNKS):
            main, low, high, src_row = parts[c]
            outs = list(
                apply_layer(
                    tick, src_row, c * rows, rows, last, (meta, main, low, high, w, bias), prev, prev_slot, emitted, emitted_aval
                )
            )
            if prev is not None or last:
                emitted = outs.pop(0)
            prev = prev_slot = None
            if not last:
                prev, left, right = outs
                prev_slot = (tick, c * rows)
                parts[c] = (hop(prev, 1, 0), hop(right, 1, 1), hop(left, 1, -1), 0)
    return emitted


def solution(mesh):
    in_specs = (
        P("section", "blk"),
        P("section", "blk", None, None, None),
        P("section", "blk", None),
        P("section", "blk"),
    )
    out_specs = P(None, "section", "blk")
    body = functools.partial(shards, mesh.shape["section"], mesh.shape["blk"])
    return jax.shard_map(body, mesh=mesh, in_specs=in_specs, out_specs=out_specs, check_vma=False)
```

```python
import functools

import jax
import jax.numpy as jnp
from jax import lax
from jax.experimental import pallas as pl
from jax.experimental.pallas import tpu as pltpu
from jax.sharding import PartitionSpec as P

BLK = 128
HALO = 4
TICKS = 8
CHUNKS = 2
VMEM = pl.BlockSpec(memory_space=pltpu.VMEM)
SMEM = pl.BlockSpec(memory_space=pltpu.SMEM)
ANY = pl.BlockSpec(memory_space=pl.ANY)


def load_kernel(blks, state, w, bias, indices, state_out, w_out, bias_out, meta, raw, sems):
    copies = [
        pltpu.make_async_copy(src, dst, sems.at[i])
        for i, (src, dst) in enumerate(((indices, raw), (state, state_out), (bias, bias_out), (w, w_out)))
    ]
    for copy in copies:
        copy.start()
    nzb, brs = indices.shape
    columns = brs * blks
    start = lax.axis_index("blk") * brs - HALO
    meta[brs * nzb] = lax.axis_index("section")
    meta[brs * nzb + 1] = lax.axis_index("blk") % 2
    copies[0].wait()

    @pl.loop(0, brs)
    def _(i):
        for k in range(nzb):
            col = raw[k, i] - start
            col = jnp.where(col < 0, col + columns, col)
            meta[i * nzb + k] = jnp.where(col >= columns, col - columns, col) * BLK

    for copy in copies[1:]:
        copy.wait()


def load(blks, state, w, bias, indices):
    arrays = (state, w, bias)
    return pl.pallas_call(
        functools.partial(load_kernel, blks),
        out_shape=(
            *(pltpu.VMEM(a.shape, a.dtype) for a in arrays),
            pltpu.SMEM((indices.size + 2,), jnp.int32),
        ),
        in_specs=[ANY] * 4,
        out_specs=(VMEM,) * 3 + (SMEM,),
        scratch_shapes=[pltpu.SMEM(indices.shape, jnp.int32), pltpu.SemaphoreType.DMA((4,))],
        compiler_params=pltpu.CompilerParams(vmem_limit_bytes=16 * 1024 * 1024),
        cost_estimate=pl.CostEstimate(flops=0, bytes_accessed=w.size * 2, transcendentals=0),
        name="load",
    )(*(pltpu.with_memory_space_constraint(a, pltpu.HBM) for a in (*arrays, indices)))


def layer_kernel(tick, src_row, rows, brs, nzb, own_slot, prev_slot, aliased, *refs):
    refs = list(refs)
    meta, main, across, inside, w, bias = refs[:6]
    del refs[:6]
    prev = None
    if prev_slot is not None:
        prev = refs.pop(0)
    if aliased:
        refs.pop(0)
    emitted = refs.pop(0) if prev_slot is not None or own_slot is not None else None
    outer = None
    if own_slot is None:
        out, outer, xbuf, sems = refs
    else:
        out, xbuf, sems = refs
    edge = HALO * BLK
    width = brs * BLK

    def write(src, slot, first, count, sem):
        where = (slice(None), pl.ds(first * BLK, count * BLK))
        slot_tick, row = slot
        return pltpu.make_async_copy(
            src.at[where], emitted.at[slot_tick, pl.ds(row, rows), pl.ds(first * BLK, count * BLK)], sem
        )

    pieces = 4
    own = []
    if own_slot is not None:
        own = [write(out, own_slot, n * brs // pieces, brs // pieces, sems.at[1 + n]) for n in range(pieces)]
    if prev is not None:
        before = write(prev, prev_slot, 0, brs, sems.at[0])
        before.start()
    live = meta[brs * nzb] >= tick
    odd = meta[brs * nzb + 1]

    @pl.when(live)
    def _():
        src = pl.ds(src_row, rows)
        xbuf[:, edge : edge + width] = main[src, :]
        xbuf[:, pl.ds(pl.multiple_of(odd * (edge + width), BLK), edge)] = across[src, :]
        xbuf[:, pl.ds(pl.multiple_of((1 - odd) * (edge + width), BLK), edge)] = inside[src, :]
        for i in range(brs):
            picked = jnp.concatenate(
                [xbuf[:, pl.ds(pl.multiple_of(meta[i * nzb + k], BLK), BLK)] for k in range(nzb)], axis=1
            )
            cols = pl.ds(i * BLK, BLK)
            summed = jnp.dot(picked, w[i], preferred_element_type=jnp.float32) + bias[:, cols]
            made = jnp.maximum(summed, 0.0).astype(jnp.bfloat16)
            out[:, cols] = made
            if own and (i + 1) % (brs // pieces) == 0:
                own[i // (brs // pieces)].start()
        if outer is not None:
            outer[...] = out[:, pl.ds(pl.multiple_of(odd * (width - edge), BLK), edge)]

    @pl.when(jnp.logical_not(live))
    def _():
        out[...] = jnp.zeros_like(out)
        if outer is not None:
            outer[...] = jnp.zeros_like(outer)
        for copy in own:
            copy.start()

    if prev is not None:
        before.wait()
    for copy in own:
        copy.wait()


def apply_layer(tick, src_row, row, rows, last, operands, prev, prev_slot, emitted, emitted_aval):
    meta, main, across, inside, w, bias = operands
    brs, depth = w.shape[:2]
    nzb = depth // BLK
    width = brs * BLK
    edge = HALO * BLK
    args = [
        pltpu.with_memory_space_constraint(meta, pltpu.SMEM),
        *(pltpu.with_memory_space_constraint(a, pltpu.VMEM) for a in (main, across, inside, w, bias)),
    ]
    specs = [SMEM] + [VMEM] * 5
    out_shape = []
    out_specs = []
    scratch = [
        pltpu.VMEM((rows, width + 2 * edge), jnp.bfloat16),
        pltpu.SemaphoreType.DMA((5,)),
    ]
    aliases = {}
    if prev is not None:
        args.append(pltpu.with_memory_space_constraint(prev, pltpu.VMEM))
        specs.append(VMEM)
    if emitted is not None:
        aliases = {len(args): 0}
        args.append(emitted)
        specs.append(ANY)
    if prev is not None or last:
        out_shape.append(emitted_aval)
        out_specs.append(ANY)
    if last:
        scratch.insert(0, pltpu.VMEM((rows, width), jnp.bfloat16))
    else:
        out_shape += [pltpu.VMEM((rows, cols), jnp.bfloat16) for cols in (width, edge)]
        out_specs += [VMEM] * 2
    body = functools.partial(
        layer_kernel, tick, src_row, rows, brs, nzb, (tick, row) if last else None, prev_slot, emitted is not None
    )
    return pl.pallas_call(
        body,
        out_shape=tuple(out_shape),
        in_specs=specs,
        out_specs=tuple(out_specs),
        scratch_shapes=scratch,
        input_output_aliases=aliases,
        compiler_params=pltpu.CompilerParams(vmem_limit_bytes=8 * 1024 * 1024),
        cost_estimate=pl.CostEstimate(
            flops=14 * rows * brs * nzb * BLK * BLK, bytes_accessed=14 * w.size, transcendentals=0
        ),
        name=f"layer_t{tick}_r{row}",
    )(*args)


def edge_kernel(meta, main, after, edge):
    del after
    odd = meta[meta.shape[0] - 1]
    width = main.shape[1]
    edge[...] = main[:, pl.ds(pl.multiple_of((1 - odd) * (width - HALO * BLK), BLK), HALO * BLK)]


def inner_edge(meta, main, after):
    return pl.pallas_call(
        edge_kernel,
        out_shape=pltpu.VMEM((main.shape[0], HALO * BLK), main.dtype),
        in_specs=[SMEM, VMEM, ANY],
        out_specs=VMEM,
        compiler_params=pltpu.CompilerParams(vmem_limit_bytes=1024 * 1024),
        name="edge",
    )(
        pltpu.with_memory_space_constraint(meta, pltpu.SMEM),
        pltpu.with_memory_space_constraint(main, pltpu.VMEM),
        after,
    )


def shards(sections, blks, pending_groups, coefficient_tiles, source_block_indices, additive_offsets):
    block_rows, nzb = coefficient_tiles.shape[1:3]
    height, width = pending_groups.shape
    rows = height // CHUNKS
    edge = HALO * BLK
    emitted_aval = jax.ShapeDtypeStruct((TICKS, height, width), jnp.bfloat16)

    def hop(values, step, place):
        pairs = [
            (s * blks + i, (s + step) % sections * blks + place(i) % blks)
            for s in range(sections)
            for i in range(blks)
        ]
        return lax.ppermute(values, ("section", "blk"), pairs)

    def across(i):
        return i + 1 if i % 2 else i - 1

    def inside(i):
        return i - 1 if i % 2 else i + 1

    odd = lax.axis_index("blk") % 2
    outer = lax.dynamic_slice_in_dim(pending_groups, odd * (width - edge), edge, axis=1)
    inner = lax.dynamic_slice_in_dim(pending_groups, (1 - odd) * (width - edge), edge, axis=1)
    far, near = hop(outer, 0, across), hop(inner, 0, inside)
    state, w, bias, meta = load(
        blks,
        pending_groups,
        coefficient_tiles.reshape(block_rows, nzb * BLK, BLK),
        additive_offsets,
        source_block_indices[0].T,
    )
    parts = [(state, far)] * CHUNKS
    emitted = prev = sent = prev_slot = None
    for tick in range(TICKS):
        last = tick + 1 == TICKS
        for c in range(CHUNKS):
            main, far = parts[c]
            src_row = c * rows
            if tick > 0:
                near = hop(inner_edge(meta, main, emitted if sent is None else sent), 0, inside)
                src_row = 0
            outs = list(
                apply_layer(
                    tick, src_row, c * rows, rows, last, (meta, main, far, near, w, bias), prev, prev_slot, emitted, emitted_aval
                )
            )
            if prev is not None or last:
                emitted = outs.pop(0)
            prev = prev_slot = None
            if not last:
                prev, outer = outs
                prev_slot = (tick, c * rows)
                sent = hop(outer, 1, across)
                parts[c] = (hop(prev, 1, lambda i: i), sent)
    return emitted


def solution(mesh):
    in_specs = (
        P("section", "blk"),
        P("section", "blk", None, None, None),
        P("section", "blk", None),
        P("section", "blk"),
    )
    out_specs = P(None, "section", "blk")
    body = functools.partial(shards, mesh.shape["section"], mesh.shape["blk"])
    return jax.shard_map(body, mesh=mesh, in_specs=in_specs, out_specs=out_specs, check_vma=False)
```

```python
import functools

import jax
import jax.numpy as jnp
from jax import lax
from jax.experimental import pallas as pl
from jax.experimental.pallas import tpu as pltpu
from jax.sharding import PartitionSpec as P

BLK = 128
HALO = 4
TICKS = 8
CHUNKS = 2
VMEM = pl.BlockSpec(memory_space=pltpu.VMEM)
SMEM = pl.BlockSpec(memory_space=pltpu.SMEM)
ANY = pl.BlockSpec(memory_space=pl.ANY)


def load_kernel(blks, state, w, bias, indices, state_out, w_out, bias_out, meta, raw, sems):
    copies = [
        pltpu.make_async_copy(src, dst, sems.at[i])
        for i, (src, dst) in enumerate(((indices, raw), (state, state_out), (bias, bias_out), (w, w_out)))
    ]
    for copy in copies:
        copy.start()
    nzb, brs = indices.shape
    columns = brs * blks
    start = lax.axis_index("blk") * brs - HALO
    meta[brs * nzb] = lax.axis_index("section")
    meta[brs * nzb + 1] = lax.axis_index("blk") % 2
    copies[0].wait()

    @pl.loop(0, brs)
    def _(i):
        for k in range(nzb):
            col = raw[k, i] - start
            col = jnp.where(col < 0, col + columns, col)
            meta[i * nzb + k] = jnp.where(col >= columns, col - columns, col) * BLK

    for copy in copies[1:]:
        copy.wait()


def load(blks, state, w, bias, indices):
    arrays = (state, w, bias)
    return pl.pallas_call(
        functools.partial(load_kernel, blks),
        out_shape=(
            *(pltpu.VMEM(a.shape, a.dtype) for a in arrays),
            pltpu.SMEM((indices.size + 2,), jnp.int32),
        ),
        in_specs=[ANY] * 4,
        out_specs=(VMEM,) * 3 + (SMEM,),
        scratch_shapes=[pltpu.SMEM(indices.shape, jnp.int32), pltpu.SemaphoreType.DMA((4,))],
        compiler_params=pltpu.CompilerParams(vmem_limit_bytes=16 * 1024 * 1024),
        cost_estimate=pl.CostEstimate(flops=0, bytes_accessed=w.size * 2, transcendentals=0),
        name="load",
    )(*(pltpu.with_memory_space_constraint(a, pltpu.HBM) for a in (*arrays, indices)))


def layer_kernel(tick, src_row, rows, brs, nzb, own_slot, prev_slot, aliased, *refs):
    refs = list(refs)
    meta, main, across, inside, w, bias = refs[:6]
    del refs[:6]
    prev = None
    if prev_slot is not None:
        prev = refs.pop(0)
    if aliased:
        refs.pop(0)
    emitted = refs.pop(0) if prev_slot is not None or own_slot is not None else None
    outer = None
    if own_slot is None:
        out, outer, xbuf, sems = refs
    else:
        out, xbuf, sems = refs
    edge = HALO * BLK
    width = brs * BLK

    def write(src, slot, first, count, sem):
        where = (slice(None), pl.ds(first * BLK, count * BLK))
        slot_tick, row = slot
        return pltpu.make_async_copy(
            src.at[where], emitted.at[slot_tick, pl.ds(row, rows), pl.ds(first * BLK, count * BLK)], sem
        )

    pieces = 4
    own = []
    if own_slot is not None:
        own = [write(out, own_slot, n * brs // pieces, brs // pieces, sems.at[1 + n]) for n in range(pieces)]
    if prev is not None:
        before = write(prev, prev_slot, 0, brs, sems.at[0])
        before.start()
    live = meta[brs * nzb] >= tick
    odd = meta[brs * nzb + 1]

    @pl.when(live)
    def _():
        src = pl.ds(src_row, rows)
        xbuf[:, edge : edge + width] = main[src, :]
        xbuf[:, pl.ds(pl.multiple_of(odd * (edge + width), BLK), edge)] = across[src, :]
        xbuf[:, pl.ds(pl.multiple_of((1 - odd) * (edge + width), BLK), edge)] = inside[src, :]
        for i in range(brs):
            picked = jnp.concatenate(
                [xbuf[:, pl.ds(pl.multiple_of(meta[i * nzb + k], BLK), BLK)] for k in range(nzb)], axis=1
            )
            cols = pl.ds(i * BLK, BLK)
            summed = jnp.dot(picked, w[i], preferred_element_type=jnp.float32) + bias[:, cols]
            made = jnp.maximum(summed, 0.0).astype(jnp.bfloat16)
            out[:, cols] = made
            if own and (i + 1) % (brs // pieces) == 0:
                own[i // (brs // pieces)].start()
        if outer is not None:
            outer[...] = out[:, pl.ds(pl.multiple_of(odd * (width - edge), BLK), edge)]

    @pl.when(jnp.logical_not(live))
    def _():
        out[...] = jnp.zeros_like(out)
        if outer is not None:
            outer[...] = jnp.zeros_like(outer)
        for copy in own:
            copy.start()

    if prev is not None:
        before.wait()
    for copy in own:
        copy.wait()


def apply_layer(tick, src_row, row, rows, last, operands, prev, prev_slot, emitted, emitted_aval):
    meta, main, across, inside, w, bias = operands
    brs, depth = w.shape[:2]
    nzb = depth // BLK
    width = brs * BLK
    edge = HALO * BLK
    args = [
        pltpu.with_memory_space_constraint(meta, pltpu.SMEM),
        *(pltpu.with_memory_space_constraint(a, pltpu.VMEM) for a in (main, across, inside, w, bias)),
    ]
    specs = [SMEM] + [VMEM] * 5
    out_shape = []
    out_specs = []
    scratch = [
        pltpu.VMEM((rows, width + 2 * edge), jnp.bfloat16),
        pltpu.SemaphoreType.DMA((5,)),
    ]
    aliases = {}
    if prev is not None:
        args.append(pltpu.with_memory_space_constraint(prev, pltpu.VMEM))
        specs.append(VMEM)
    if emitted is not None:
        aliases = {len(args): 0}
        args.append(emitted)
        specs.append(ANY)
    if prev is not None or last:
        out_shape.append(emitted_aval)
        out_specs.append(ANY)
    if last:
        scratch.insert(0, pltpu.VMEM((rows, width), jnp.bfloat16))
    else:
        out_shape += [pltpu.VMEM((rows, cols), jnp.bfloat16) for cols in (width, edge)]
        out_specs += [VMEM] * 2
    body = functools.partial(
        layer_kernel, tick, src_row, rows, brs, nzb, (tick, row) if last else None, prev_slot, emitted is not None
    )
    return pl.pallas_call(
        body,
        out_shape=tuple(out_shape),
        in_specs=specs,
        out_specs=tuple(out_specs),
        scratch_shapes=scratch,
        input_output_aliases=aliases,
        compiler_params=pltpu.CompilerParams(vmem_limit_bytes=8 * 1024 * 1024),
        cost_estimate=pl.CostEstimate(
            flops=18 * rows * brs * nzb * BLK * BLK, bytes_accessed=18 * w.size, transcendentals=0
        ),
        name=f"layer_t{tick}_r{row}",
    )(*args)


def edge_kernel(meta, main, far, after, edge):
    del far, after
    odd = meta[meta.shape[0] - 1]
    width = main.shape[1]
    edge[...] = main[:, pl.ds(pl.multiple_of((1 - odd) * (width - HALO * BLK), BLK), HALO * BLK)]


def inner_edge(meta, main, far, after):
    return pl.pallas_call(
        edge_kernel,
        out_shape=pltpu.VMEM((main.shape[0], HALO * BLK), main.dtype),
        in_specs=[SMEM, VMEM, ANY, ANY],
        out_specs=VMEM,
        compiler_params=pltpu.CompilerParams(vmem_limit_bytes=1024 * 1024),
        name="edge",
    )(
        pltpu.with_memory_space_constraint(meta, pltpu.SMEM),
        pltpu.with_memory_space_constraint(main, pltpu.VMEM),
        far,
        after,
    )


def shards(sections, blks, pending_groups, coefficient_tiles, source_block_indices, additive_offsets):
    block_rows, nzb = coefficient_tiles.shape[1:3]
    height, width = pending_groups.shape
    rows = height // CHUNKS
    edge = HALO * BLK
    emitted_aval = jax.ShapeDtypeStruct((TICKS, height, width), jnp.bfloat16)

    def hop(values, step, place):
        pairs = [
            (s * blks + i, (s + step) % sections * blks + place(i) % blks)
            for s in range(sections)
            for i in range(blks)
        ]
        return lax.ppermute(values, ("section", "blk"), pairs)

    def across(i):
        return i + 1 if i % 2 else i - 1

    def inside(i):
        return i - 1 if i % 2 else i + 1

    odd = lax.axis_index("blk") % 2
    outer = lax.dynamic_slice_in_dim(pending_groups, odd * (width - edge), edge, axis=1)
    inner = lax.dynamic_slice_in_dim(pending_groups, (1 - odd) * (width - edge), edge, axis=1)
    far, near = hop(outer, 0, across), hop(inner, 0, inside)
    state, w, bias, meta = load(
        blks,
        pending_groups,
        coefficient_tiles.reshape(block_rows, nzb * BLK, BLK),
        additive_offsets,
        source_block_indices[0].T,
    )
    parts = [(state, far)] * CHUNKS
    emitted = prev = prev_slot = made = None
    for tick in range(TICKS):
        last = tick + 1 == TICKS
        for c in range(CHUNKS):
            main, far = parts[c]
            src_row = c * rows
            if tick > 0:
                near = hop(inner_edge(meta, main, far, made), 0, inside)
                src_row = 0
            outs = list(
                apply_layer(
                    tick, src_row, c * rows, rows, last, (meta, main, far, near, w, bias), prev, prev_slot, emitted, emitted_aval
                )
            )
            if prev is not None or last:
                emitted = outs.pop(0)
            prev = prev_slot = None
            if not last:
                prev, outer = outs
                made = prev
                prev_slot = (tick, c * rows)
                parts[c] = (hop(prev, 1, lambda i: i), hop(outer, 1, across))
    return emitted


def solution(mesh):
    in_specs = (
        P("section", "blk"),
        P("section", "blk", None, None, None),
        P("section", "blk", None),
        P("section", "blk"),
    )
    out_specs = P(None, "section", "blk")
    body = functools.partial(shards, mesh.shape["section"], mesh.shape["blk"])
    return jax.shard_map(body, mesh=mesh, in_specs=in_specs, out_specs=out_specs, check_vma=False)
```

```python
import functools

import jax
import jax.numpy as jnp
from jax import lax
from jax.experimental import pallas as pl
from jax.experimental.pallas import tpu as pltpu
from jax.sharding import PartitionSpec as P

BLK = 128
HALO = 4
TICKS = 8
CHUNKS = 2
VMEM = pl.BlockSpec(memory_space=pltpu.VMEM)
SMEM = pl.BlockSpec(memory_space=pltpu.SMEM)
ANY = pl.BlockSpec(memory_space=pl.ANY)


def load_kernel(blks, state, w, bias, indices, state_out, w_out, bias_out, meta, raw, sems):
    copies = [
        pltpu.make_async_copy(src, dst, sems.at[i])
        for i, (src, dst) in enumerate(((indices, raw), (state, state_out), (bias, bias_out), (w, w_out)))
    ]
    for copy in copies:
        copy.start()
    nzb, brs = indices.shape
    columns = brs * blks
    start = lax.axis_index("blk") * brs - HALO
    meta[brs * nzb] = lax.axis_index("section")
    meta[brs * nzb + 1] = lax.axis_index("blk") % 2
    copies[0].wait()

    @pl.loop(0, brs)
    def _(i):
        for k in range(nzb):
            col = raw[k, i] - start
            col = jnp.where(col < 0, col + columns, col)
            meta[i * nzb + k] = jnp.where(col >= columns, col - columns, col) * BLK

    for copy in copies[1:]:
        copy.wait()


def load(blks, state, w, bias, indices):
    arrays = (state, w, bias)
    return pl.pallas_call(
        functools.partial(load_kernel, blks),
        out_shape=(
            *(pltpu.VMEM(a.shape, a.dtype) for a in arrays),
            pltpu.SMEM((indices.size + 2,), jnp.int32),
        ),
        in_specs=[ANY] * 4,
        out_specs=(VMEM,) * 3 + (SMEM,),
        scratch_shapes=[pltpu.SMEM(indices.shape, jnp.int32), pltpu.SemaphoreType.DMA((4,))],
        compiler_params=pltpu.CompilerParams(vmem_limit_bytes=16 * 1024 * 1024),
        cost_estimate=pl.CostEstimate(flops=0, bytes_accessed=w.size * 2, transcendentals=0),
        name="load",
    )(*(pltpu.with_memory_space_constraint(a, pltpu.HBM) for a in (*arrays, indices)))


def layer_kernel(tick, src_row, rows, brs, nzb, own_slot, prev_slot, aliased, *refs):
    refs = list(refs)
    meta, main, across, inside, w, bias = refs[:6]
    del refs[:6]
    prev = None
    if prev_slot is not None:
        prev = refs.pop(0)
    if aliased:
        refs.pop(0)
    emitted = refs.pop(0) if prev_slot is not None or own_slot is not None else None
    outer = None
    if own_slot is None:
        out, outer, xbuf, sems = refs
    else:
        out, xbuf, sems = refs
    edge = HALO * BLK
    width = brs * BLK

    def write(src, slot, first, count, sem):
        where = (slice(None), pl.ds(first * BLK, count * BLK))
        slot_tick, row = slot
        return pltpu.make_async_copy(
            src.at[where], emitted.at[slot_tick, pl.ds(row, rows), pl.ds(first * BLK, count * BLK)], sem
        )

    pieces = 4
    own = []
    if own_slot is not None:
        own = [write(out, own_slot, n * brs // pieces, brs // pieces, sems.at[1 + n]) for n in range(pieces)]
    if prev is not None:
        before = write(prev, prev_slot, 0, brs, sems.at[0])
        before.start()
    live = meta[brs * nzb] >= tick
    odd = meta[brs * nzb + 1]

    @pl.when(live)
    def _():
        src = pl.ds(src_row, rows)
        xbuf[:, edge : edge + width] = main[src, :]
        xbuf[:, pl.ds(pl.multiple_of(odd * (edge + width), BLK), edge)] = across[src, :]
        xbuf[:, pl.ds(pl.multiple_of((1 - odd) * (edge + width), BLK), edge)] = inside[src, :]
        for i in range(brs):
            picked = jnp.concatenate(
                [xbuf[:, pl.ds(pl.multiple_of(meta[i * nzb + k], BLK), BLK)] for k in range(nzb)], axis=1
            )
            cols = pl.ds(i * BLK, BLK)
            summed = jnp.dot(picked, w[i], preferred_element_type=jnp.float32) + bias[:, cols]
            made = jnp.maximum(summed, 0.0).astype(jnp.bfloat16)
            out[:, cols] = made
            if own and (i + 1) % (brs // pieces) == 0:
                own[i // (brs // pieces)].start()
        if outer is not None:
            outer[...] = out[:, pl.ds(pl.multiple_of(odd * (width - edge), BLK), edge)]

    @pl.when(jnp.logical_not(live))
    def _():
        out[...] = jnp.zeros_like(out)
        if outer is not None:
            outer[...] = jnp.zeros_like(outer)
        for copy in own:
            copy.start()

    if prev is not None:
        before.wait()
    for copy in own:
        copy.wait()


def apply_layer(tick, src_row, row, rows, last, operands, prev, prev_slot, emitted, emitted_aval):
    meta, main, across, inside, w, bias = operands
    brs, depth = w.shape[:2]
    nzb = depth // BLK
    width = brs * BLK
    edge = HALO * BLK
    args = [
        pltpu.with_memory_space_constraint(meta, pltpu.SMEM),
        *(pltpu.with_memory_space_constraint(a, pltpu.VMEM) for a in (main, across, inside, w, bias)),
    ]
    specs = [SMEM] + [VMEM] * 5
    out_shape = []
    out_specs = []
    scratch = [
        pltpu.VMEM((rows, width + 2 * edge), jnp.bfloat16),
        pltpu.SemaphoreType.DMA((5,)),
    ]
    aliases = {}
    if prev is not None:
        args.append(pltpu.with_memory_space_constraint(prev, pltpu.VMEM))
        specs.append(VMEM)
    if emitted is not None:
        aliases = {len(args): 0}
        args.append(emitted)
        specs.append(ANY)
    if prev is not None or last:
        out_shape.append(emitted_aval)
        out_specs.append(ANY)
    if last:
        scratch.insert(0, pltpu.VMEM((rows, width), jnp.bfloat16))
    else:
        out_shape += [pltpu.VMEM((rows, cols), jnp.bfloat16) for cols in (width, edge)]
        out_specs += [VMEM] * 2
    body = functools.partial(
        layer_kernel, tick, src_row, rows, brs, nzb, (tick, row) if last else None, prev_slot, emitted is not None
    )
    return pl.pallas_call(
        body,
        out_shape=tuple(out_shape),
        in_specs=specs,
        out_specs=tuple(out_specs),
        scratch_shapes=scratch,
        input_output_aliases=aliases,
        compiler_params=pltpu.CompilerParams(vmem_limit_bytes=8 * 1024 * 1024),
        cost_estimate=pl.CostEstimate(
            flops=18 * rows * brs * nzb * BLK * BLK, bytes_accessed=18 * w.size, transcendentals=0
        ),
        name=f"layer_t{tick}_r{row}",
    )(*args)


def edge_kernel(meta, main, far, after, edge):
    del far, after
    odd = meta[meta.shape[0] - 1]
    width = main.shape[1]
    edge[...] = main[:, pl.ds(pl.multiple_of((1 - odd) * (width - HALO * BLK), BLK), HALO * BLK)]


def inner_edge(meta, main, far, after):
    return pl.pallas_call(
        edge_kernel,
        out_shape=pltpu.VMEM((main.shape[0], HALO * BLK), main.dtype),
        in_specs=[SMEM, VMEM, ANY, ANY],
        out_specs=VMEM,
        compiler_params=pltpu.CompilerParams(vmem_limit_bytes=1024 * 1024),
        name="edge",
    )(
        pltpu.with_memory_space_constraint(meta, pltpu.SMEM),
        pltpu.with_memory_space_constraint(main, pltpu.VMEM),
        far,
        after,
    )


def shards(sections, blks, pending_groups, coefficient_tiles, source_block_indices, additive_offsets):
    block_rows, nzb = coefficient_tiles.shape[1:3]
    height, width = pending_groups.shape
    rows = height // CHUNKS
    edge = HALO * BLK
    emitted_aval = jax.ShapeDtypeStruct((TICKS, height, width), jnp.bfloat16)

    def hop(values, place, tick=None):
        pairs = []
        for s in range(sections):
            target = s
            if tick is not None and s >= tick:
                target = s + 1 if s + 1 < sections else tick
            for i in range(blks):
                moved = place(i) % blks if tick is None or s >= tick else i
                pairs.append((s * blks + i, target * blks + moved))
        return lax.ppermute(values, ("section", "blk"), pairs)

    def same(i):
        return i

    def across(i):
        return i + 1 if i % 2 else i - 1

    def inside(i):
        return i - 1 if i % 2 else i + 1

    odd = lax.axis_index("blk") % 2
    outer = lax.dynamic_slice_in_dim(pending_groups, odd * (width - edge), edge, axis=1)
    inner = lax.dynamic_slice_in_dim(pending_groups, (1 - odd) * (width - edge), edge, axis=1)
    far, near = hop(outer, across), hop(inner, inside)
    state, w, bias, meta = load(
        blks,
        pending_groups,
        coefficient_tiles.reshape(block_rows, nzb * BLK, BLK),
        additive_offsets,
        source_block_indices[0].T,
    )
    parts = [(state, far)] * CHUNKS
    emitted = prev = prev_slot = made = None
    for tick in range(TICKS):
        last = tick + 1 == TICKS
        for c in range(CHUNKS):
            main, far = parts[c]
            src_row = c * rows
            if tick > 0:
                near = hop(inner_edge(meta, main, far, made), inside)
                src_row = 0
            outs = list(
                apply_layer(
                    tick, src_row, c * rows, rows, last, (meta, main, far, near, w, bias), prev, prev_slot, emitted, emitted_aval
                )
            )
            if prev is not None or last:
                emitted = outs.pop(0)
            prev = prev_slot = None
            if not last:
                prev, outer = outs
                made = prev
                prev_slot = (tick, c * rows)
                parts[c] = (hop(prev, same, tick), hop(outer, across, tick))
    return emitted


def solution(mesh):
    in_specs = (
        P("section", "blk"),
        P("section", "blk", None, None, None),
        P("section", "blk", None),
        P("section", "blk"),
    )
    out_specs = P(None, "section", "blk")
    body = functools.partial(shards, mesh.shape["section"], mesh.shape["blk"])
    return jax.shard_map(body, mesh=mesh, in_specs=in_specs, out_specs=out_specs, check_vma=False)
```

```python
import functools

import jax
import jax.numpy as jnp
from jax import lax
from jax.experimental import pallas as pl
from jax.experimental.pallas import tpu as pltpu
from jax.sharding import PartitionSpec as P

BLK = 128
HALO = 4
TICKS = 8
CHUNKS = 2
VMEM = pl.BlockSpec(memory_space=pltpu.VMEM)
SMEM = pl.BlockSpec(memory_space=pltpu.SMEM)
ANY = pl.BlockSpec(memory_space=pl.ANY)


def load_kernel(blks, state, w, bias, indices, state_out, w_out, bias_out, meta, raw, sems):
    copies = [
        pltpu.make_async_copy(src, dst, sems.at[i])
        for i, (src, dst) in enumerate(
            ((indices, raw), (state, state_out), (bias, bias_out), (w.at[: w_out.shape[0]], w_out))
        )
    ]
    for copy in copies:
        copy.start()
    nzb, brs = indices.shape
    columns = brs * blks
    start = lax.axis_index("blk") * brs - HALO
    meta[brs * nzb] = lax.axis_index("section")
    copies[0].wait()

    @pl.loop(0, brs)
    def _(i):
        for k in range(nzb):
            col = raw[k, i] - start
            col = jnp.where(col < 0, col + columns, col)
            meta[i * nzb + k] = jnp.where(col >= columns, col - columns, col) * BLK

    for copy in copies[1:]:
        copy.wait()


def load(blks, state, w, bias, indices):
    arrays = (state, w, bias)
    return pl.pallas_call(
        functools.partial(load_kernel, blks),
        out_shape=(
            pltpu.VMEM(state.shape, state.dtype),
            pltpu.VMEM((w.shape[0] // 2, *w.shape[1:]), w.dtype),
            pltpu.VMEM(bias.shape, bias.dtype),
            pltpu.SMEM((indices.size + 1,), jnp.int32),
        ),
        in_specs=[ANY] * 4,
        out_specs=(VMEM,) * 3 + (SMEM,),
        scratch_shapes=[pltpu.SMEM(indices.shape, jnp.int32), pltpu.SemaphoreType.DMA((4,))],
        compiler_params=pltpu.CompilerParams(vmem_limit_bytes=16 * 1024 * 1024),
        cost_estimate=pl.CostEstimate(flops=0, bytes_accessed=w.size * 2, transcendentals=0),
        name="load",
    )(*(pltpu.with_memory_space_constraint(a, pltpu.HBM) for a in (*arrays, indices)))


def layer_kernel(tick, src_row, rows, brs, nzb, own_slot, prev_slot, aliased, *refs):
    refs = list(refs)
    meta, main, low, high, w_early, w_late, bias = refs[:7]
    del refs[:7]
    prev = refs.pop(0) if prev_slot is not None else None
    if aliased:
        refs.pop(0)
    emitted = refs.pop(0) if prev_slot is not None or own_slot is not None else None
    left = right = None
    late = None
    early = w_early.shape[0]
    if prev_slot is None and own_slot is None:
        out, left, right, loaded, xbuf, sems = refs
        late = pltpu.make_async_copy(w_late.at[early:], loaded, sems.at[0])
        w_late = loaded
        late.start()
    elif own_slot is None:
        out, left, right, xbuf, sems = refs
    else:
        out, xbuf, sems = refs
    edge = HALO * BLK
    width = brs * BLK

    def write(src, slot, first, count, sem):
        where = (slice(None), pl.ds(first * BLK, count * BLK))
        slot_tick, row = slot
        return pltpu.make_async_copy(
            src.at[where], emitted.at[slot_tick, pl.ds(row, rows), pl.ds(first * BLK, count * BLK)], sem
        )

    pieces = 4
    own = []
    if own_slot is not None:
        own = [write(out, own_slot, n * brs // pieces, brs // pieces, sems.at[1 + n]) for n in range(pieces)]
    if prev is not None:
        before = write(prev, prev_slot, 0, brs, sems.at[0])
        before.start()
    live = meta[brs * nzb] >= tick

    def compute():
        src = pl.ds(src_row, rows)
        xbuf[:, 0:edge] = low[src, :]
        xbuf[:, edge : edge + width] = main[src, :]
        xbuf[:, edge + width : edge + width + edge] = high[src, :]
        for i in range(brs):
            if late is not None and i == early:
                late.wait()
            picked = jnp.concatenate(
                [xbuf[:, pl.ds(pl.multiple_of(meta[i * nzb + k], BLK), BLK)] for k in range(nzb)], axis=1
            )
            cols = pl.ds(i * BLK, BLK)
            w = w_early[i] if i < early else w_late[i - early]
            summed = jnp.dot(picked, w, preferred_element_type=jnp.float32) + bias[:, cols]
            made = jnp.maximum(summed, 0.0).astype(jnp.bfloat16)
            out[:, cols] = made
            if left is not None and i < HALO:
                left[:, cols] = made
            if right is not None and i >= brs - HALO:
                right[:, pl.ds((i - brs + HALO) * BLK, BLK)] = made
            if own and (i + 1) % (brs // pieces) == 0:
                own[i // (brs // pieces)].start()

    def clear():
        out[...] = jnp.zeros_like(out)
        if left is not None:
            left[...] = jnp.zeros_like(left)
            right[...] = jnp.zeros_like(right)
        for copy in own:
            copy.start()

    if tick == 0:
        compute()
    else:
        pl.when(live)(compute)
        pl.when(jnp.logical_not(live))(clear)
    if prev is not None:
        before.wait()
    for copy in own:
        copy.wait()


def apply_layer(tick, src_row, row, rows, last, operands, prev, prev_slot, emitted, emitted_aval):
    meta, main, low, high, w_early, w_late, bias = operands
    depth = w_early.shape[1]
    brs = bias.shape[1] // BLK
    nzb = depth // BLK
    width = brs * BLK
    edge = HALO * BLK
    args = [
        pltpu.with_memory_space_constraint(meta, pltpu.SMEM),
        *(pltpu.with_memory_space_constraint(a, pltpu.VMEM) for a in (main, low, high, w_early)),
        pltpu.with_memory_space_constraint(w_late, pltpu.VMEM if prev is not None or last else pltpu.HBM),
        pltpu.with_memory_space_constraint(bias, pltpu.VMEM),
    ]
    specs = [SMEM] + [VMEM] * 6
    if prev is None and not last:
        specs[5] = ANY
    out_shape = []
    out_specs = []
    scratch = [
        pltpu.VMEM((rows, width + 2 * edge), jnp.bfloat16),
        pltpu.SemaphoreType.DMA((5,)),
    ]
    aliases = {}
    if prev is not None:
        args.append(pltpu.with_memory_space_constraint(prev, pltpu.VMEM))
        specs.append(VMEM)
    if emitted is not None:
        aliases = {len(args): 0}
        args.append(emitted)
        specs.append(ANY)
    if prev is not None or last:
        out_shape.append(emitted_aval)
        out_specs.append(ANY)
    if last:
        scratch.insert(0, pltpu.VMEM((rows, width), jnp.bfloat16))
    else:
        out_shape += [pltpu.VMEM((rows, cols), jnp.bfloat16) for cols in (width, edge, edge)]
        out_specs += [VMEM] * 3
    if prev is None and not last:
        out_shape.append(pltpu.VMEM((brs - w_early.shape[0], depth, BLK), w_early.dtype))
        out_specs.append(VMEM)
    body = functools.partial(
        layer_kernel, tick, src_row, rows, brs, nzb, (tick, row) if last else None, prev_slot, emitted is not None
    )
    return pl.pallas_call(
        body,
        out_shape=tuple(out_shape),
        in_specs=specs,
        out_specs=tuple(out_specs),
        scratch_shapes=scratch,
        input_output_aliases=aliases,
        compiler_params=pltpu.CompilerParams(vmem_limit_bytes=8 * 1024 * 1024),
        cost_estimate=pl.CostEstimate(
            flops=20 * rows * brs * nzb * BLK * BLK, bytes_accessed=40 * w_early.size, transcendentals=0
        ),
        name=f"layer_t{tick}_r{row}",
    )(*args)


def shards(sections, blks, pending_groups, coefficient_tiles, source_block_indices, additive_offsets):
    block_rows, nzb = coefficient_tiles.shape[1:3]
    height, width = pending_groups.shape
    rows = height // CHUNKS
    edge = HALO * BLK
    emitted_aval = jax.ShapeDtypeStruct((TICKS, height, width), jnp.bfloat16)

    def hop(values, step, shift):
        pairs = [
            (s * blks + i, (s + step) % sections * blks + (i + shift) % blks)
            for s in range(sections)
            for i in range(blks)
        ]
        return lax.ppermute(values, ("section", "blk"), pairs)

    low = hop(pending_groups[:, width - edge :], 0, 1)
    high = hop(pending_groups[:, :edge], 0, -1)
    w_late = coefficient_tiles.reshape(block_rows, nzb * BLK, BLK)
    state, w_early, bias, meta = load(
        blks,
        pending_groups,
        w_late,
        additive_offsets,
        source_block_indices[0].T,
    )
    parts = [(state, low, high, c * rows) for c in range(CHUNKS)]
    emitted = prev = prev_slot = None
    for tick in range(TICKS):
        last = tick + 1 == TICKS
        for c in range(CHUNKS):
            main, low, high, src_row = parts[c]
            outs = list(
                apply_layer(
                    tick, src_row, c * rows, rows, last, (meta, main, low, high, w_early, w_late, bias), prev, prev_slot, emitted, emitted_aval
                )
            )
            if prev is not None or last:
                emitted = outs.pop(0)
            if tick == 0 and c == 0:
                w_late = outs.pop()
            prev = prev_slot = None
            if not last:
                prev, left, right = outs
                prev_slot = (tick, c * rows)
                parts[c] = (hop(prev, 1, 0), hop(right, 1, 1), hop(left, 1, -1), 0)
    return emitted


def solution(mesh):
    in_specs = (
        P("section", "blk"),
        P("section", "blk", None, None, None),
        P("section", "blk", None),
        P("section", "blk"),
    )
    out_specs = P(None, "section", "blk")
    body = functools.partial(shards, mesh.shape["section"], mesh.shape["blk"])
    return jax.shard_map(body, mesh=mesh, in_specs=in_specs, out_specs=out_specs, check_vma=False)
```

```python
import functools

import jax
import jax.numpy as jnp
from jax import lax
from jax.experimental import pallas as pl
from jax.experimental.pallas import tpu as pltpu
from jax.sharding import PartitionSpec as P

BLK = 128
HALO = 4
TICKS = 8
CHUNKS = 2
VMEM = pl.BlockSpec(memory_space=pltpu.VMEM)
SMEM = pl.BlockSpec(memory_space=pltpu.SMEM)
ANY = pl.BlockSpec(memory_space=pl.ANY)


def load_kernel(blks, state, w, bias, indices, state_out, w_out, bias_out, meta, raw, sems):
    copies = [
        pltpu.make_async_copy(src, dst, sems.at[i])
        for i, (src, dst) in enumerate(((indices, raw), (state, state_out), (bias, bias_out), (w, w_out)))
    ]
    for copy in copies:
        copy.start()
    nzb, brs = indices.shape
    columns = brs * blks
    start = lax.axis_index("blk") * brs - HALO
    meta[brs * nzb] = lax.axis_index("section")
    meta[brs * nzb + 1] = lax.axis_index("blk") % 2
    copies[0].wait()

    @pl.loop(0, brs)
    def _(i):
        for k in range(nzb):
            col = raw[k, i] - start
            col = jnp.where(col < 0, col + columns, col)
            meta[i * nzb + k] = jnp.where(col >= columns, col - columns, col) * BLK

    for copy in copies[1:]:
        copy.wait()


def load(blks, state, w, bias, indices):
    arrays = (state, w, bias)
    return pl.pallas_call(
        functools.partial(load_kernel, blks),
        out_shape=(
            *(pltpu.VMEM(a.shape, a.dtype) for a in arrays),
            pltpu.SMEM((indices.size + 2,), jnp.int32),
        ),
        in_specs=[ANY] * 4,
        out_specs=(VMEM,) * 3 + (SMEM,),
        scratch_shapes=[pltpu.SMEM(indices.shape, jnp.int32), pltpu.SemaphoreType.DMA((4,))],
        compiler_params=pltpu.CompilerParams(vmem_limit_bytes=16 * 1024 * 1024),
        cost_estimate=pl.CostEstimate(flops=0, bytes_accessed=w.size * 2, transcendentals=0),
        name="load",
    )(*(pltpu.with_memory_space_constraint(a, pltpu.HBM) for a in (*arrays, indices)))


def layer_kernel(tick, src_row, rows, brs, nzb, own_slot, prev_slot, aliased, *refs):
    refs = list(refs)
    meta, main, across = refs[:3]
    del refs[:3]
    inside = refs.pop(0) if tick == 0 else None
    w, bias = refs[:2]
    del refs[:2]
    prev = None
    if prev_slot is not None:
        prev = refs.pop(0)
    if aliased:
        refs.pop(0)
    emitted = refs.pop(0) if prev_slot is not None or own_slot is not None else None
    outer = inner = None
    if own_slot is None:
        out, outer, inner, xbuf, sems = refs
    else:
        out, xbuf, sems = refs
    edge = HALO * BLK
    width = brs * BLK

    def write(src, slot, first, count, sem):
        where = (slice(None), pl.ds(first * BLK, count * BLK))
        slot_tick, row = slot
        return pltpu.make_async_copy(
            src.at[where], emitted.at[slot_tick, pl.ds(row, rows), pl.ds(first * BLK, count * BLK)], sem
        )

    pieces = 4
    own = []
    if own_slot is not None:
        own = [write(out, own_slot, n * brs // pieces, brs // pieces, sems.at[1 + n]) for n in range(pieces)]
    if prev is not None:
        before = write(prev, prev_slot, 0, brs, sems.at[0])
        before.start()
    live = meta[brs * nzb] >= tick
    odd = meta[brs * nzb + 1]

    @pl.when(live)
    def _():
        src = pl.ds(src_row, rows)
        xbuf[:, edge : edge + width] = main[src, 0:width]
        xbuf[:, pl.ds(pl.multiple_of(odd * (edge + width), BLK), edge)] = across[src, :]
        xbuf[:, pl.ds(pl.multiple_of((1 - odd) * (edge + width), BLK), edge)] = (
            main[src, width : width + edge] if inside is None else inside[src, :]
        )
        for i in range(brs):
            picked = jnp.concatenate(
                [xbuf[:, pl.ds(pl.multiple_of(meta[i * nzb + k], BLK), BLK)] for k in range(nzb)], axis=1
            )
            cols = pl.ds(i * BLK, BLK)
            summed = jnp.dot(picked, w[i], preferred_element_type=jnp.float32) + bias[:, cols]
            made = jnp.maximum(summed, 0.0).astype(jnp.bfloat16)
            out[:, cols] = made
            if own and (i + 1) % (brs // pieces) == 0:
                own[i // (brs // pieces)].start()
        if outer is not None:
            outer[...] = out[:, pl.ds(pl.multiple_of(odd * (width - edge), BLK), edge)]
            inner[...] = out[:, pl.ds(pl.multiple_of((1 - odd) * (width - edge), BLK), edge)]

    @pl.when(jnp.logical_not(live))
    def _():
        out[...] = jnp.zeros_like(out)
        if outer is not None:
            outer[...] = jnp.zeros_like(outer)
            inner[...] = jnp.zeros_like(inner)
        for copy in own:
            copy.start()

    if prev is not None:
        before.wait()
    for copy in own:
        copy.wait()


def apply_layer(tick, src_row, row, rows, last, operands, prev, prev_slot, emitted, emitted_aval):
    meta, *local = operands
    w = local[-2]
    brs, depth = w.shape[:2]
    nzb = depth // BLK
    width = brs * BLK
    edge = HALO * BLK
    args = [
        pltpu.with_memory_space_constraint(meta, pltpu.SMEM),
        *(pltpu.with_memory_space_constraint(a, pltpu.VMEM) for a in local),
    ]
    specs = [SMEM] + [VMEM] * len(local)
    out_shape = []
    out_specs = []
    scratch = [
        pltpu.VMEM((rows, width + 2 * edge), jnp.bfloat16),
        pltpu.SemaphoreType.DMA((5,)),
    ]
    aliases = {}
    if prev is not None:
        args.append(pltpu.with_memory_space_constraint(prev, pltpu.VMEM))
        specs.append(VMEM)
    if emitted is not None:
        aliases = {len(args): 0}
        args.append(emitted)
        specs.append(ANY)
    if prev is not None or last:
        out_shape.append(emitted_aval)
        out_specs.append(ANY)
    if last:
        scratch.insert(0, pltpu.VMEM((rows, width), jnp.bfloat16))
    else:
        out_shape += [pltpu.VMEM((rows, cols), jnp.bfloat16) for cols in (width + edge, edge, edge)]
        out_specs += [VMEM] * 3
    body = functools.partial(
        layer_kernel, tick, src_row, rows, brs, nzb, (tick, row) if last else None, prev_slot, emitted is not None
    )
    return pl.pallas_call(
        body,
        out_shape=tuple(out_shape),
        in_specs=specs,
        out_specs=tuple(out_specs),
        scratch_shapes=scratch,
        input_output_aliases=aliases,
        compiler_params=pltpu.CompilerParams(vmem_limit_bytes=8 * 1024 * 1024),
        cost_estimate=pl.CostEstimate(
            flops=40 * rows * brs * nzb * BLK * BLK, bytes_accessed=40 * w.size, transcendentals=0
        ),
        name=f"layer_t{tick}_r{row}",
    )(*args)


def merge_kernel(near, made, merged):
    del made
    edge = near.shape[1]
    merged[:, merged.shape[1] - edge :] = near[...]


def merge(near, made):
    return pl.pallas_call(
        merge_kernel,
        out_shape=pltpu.VMEM(made.shape, made.dtype),
        in_specs=[VMEM, VMEM],
        out_specs=VMEM,
        input_output_aliases={1: 0},
        compiler_params=pltpu.CompilerParams(vmem_limit_bytes=1024 * 1024),
        name="merge",
    )(*(pltpu.with_memory_space_constraint(a, pltpu.VMEM) for a in (near, made)))


def shards(sections, blks, pending_groups, coefficient_tiles, source_block_indices, additive_offsets):
    block_rows, nzb = coefficient_tiles.shape[1:3]
    height, width = pending_groups.shape
    rows = height // CHUNKS
    edge = HALO * BLK
    emitted_aval = jax.ShapeDtypeStruct((TICKS, height, width), jnp.bfloat16)

    def hop(values, step, place):
        pairs = [
            (s * blks + i, (s + step) % sections * blks + place(i) % blks)
            for s in range(sections)
            for i in range(blks)
        ]
        return lax.ppermute(values, ("section", "blk"), pairs)

    def across(i):
        return i + 1 if i % 2 else i - 1

    def inside(i):
        return i - 1 if i % 2 else i + 1

    odd = lax.axis_index("blk") % 2
    outer = lax.dynamic_slice_in_dim(pending_groups, odd * (width - edge), edge, axis=1)
    inner = lax.dynamic_slice_in_dim(pending_groups, (1 - odd) * (width - edge), edge, axis=1)
    far, near = hop(outer, 0, across), hop(inner, 0, inside)
    state, w, bias, meta = load(
        blks,
        pending_groups,
        coefficient_tiles.reshape(block_rows, nzb * BLK, BLK),
        additive_offsets,
        source_block_indices[0].T,
    )
    parts = [(state, far, near)] * CHUNKS
    emitted = prev = prev_slot = None
    for tick in range(TICKS):
        last = tick + 1 == TICKS
        for c in range(CHUNKS):
            src_row = c * rows if tick == 0 else 0
            operands = (meta, *parts[c], w, bias)
            outs = list(
                apply_layer(tick, src_row, c * rows, rows, last, operands, prev, prev_slot, emitted, emitted_aval)
            )
            if prev is not None or last:
                emitted = outs.pop(0)
            prev = prev_slot = None
            if not last:
                made, outer, inner = outs
                prev = merge(hop(inner, 0, inside), made)
                prev_slot = (tick, c * rows)
                parts[c] = (hop(prev, 1, lambda i: i), hop(outer, 1, across))
    return emitted


def solution(mesh):
    in_specs = (
        P("section", "blk"),
        P("section", "blk", None, None, None),
        P("section", "blk", None),
        P("section", "blk"),
    )
    out_specs = P(None, "section", "blk")
    body = functools.partial(shards, mesh.shape["section"], mesh.shape["blk"])
    return jax.shard_map(body, mesh=mesh, in_specs=in_specs, out_specs=out_specs, check_vma=False)
```

```python
import functools

import jax
import jax.numpy as jnp
from jax import lax
from jax.experimental import pallas as pl
from jax.experimental.pallas import tpu as pltpu
from jax.sharding import PartitionSpec as P

BLK = 128
HALO = 4
TICKS = 8
CHUNKS = 2
VMEM = pl.BlockSpec(memory_space=pltpu.VMEM)
SMEM = pl.BlockSpec(memory_space=pltpu.SMEM)
ANY = pl.BlockSpec(memory_space=pl.ANY)


def load_kernel(blks, state, w, bias, indices, state_out, w_out, bias_out, meta, raw, sems):
    copies = [
        pltpu.make_async_copy(src, dst, sems.at[i])
        for i, (src, dst) in enumerate(((indices, raw), (state, state_out), (bias, bias_out), (w, w_out)))
    ]
    for copy in copies:
        copy.start()
    nzb, brs = indices.shape
    columns = brs * blks
    start = lax.axis_index("blk") * brs - HALO
    meta[brs * nzb] = lax.axis_index("section")
    meta[brs * nzb + 1] = lax.axis_index("blk") % 2
    copies[0].wait()

    @pl.loop(0, brs)
    def _(i):
        for k in range(nzb):
            col = raw[k, i] - start
            col = jnp.where(col < 0, col + columns, col)
            meta[i * nzb + k] = jnp.where(col >= columns, col - columns, col) * BLK

    for copy in copies[1:]:
        copy.wait()


def load(blks, state, w, bias, indices):
    arrays = (state, w, bias)
    return pl.pallas_call(
        functools.partial(load_kernel, blks),
        out_shape=(
            *(pltpu.VMEM(a.shape, a.dtype) for a in arrays),
            pltpu.SMEM((indices.size + 2,), jnp.int32),
        ),
        in_specs=[ANY] * 4,
        out_specs=(VMEM,) * 3 + (SMEM,),
        scratch_shapes=[pltpu.SMEM(indices.shape, jnp.int32), pltpu.SemaphoreType.DMA((4,))],
        compiler_params=pltpu.CompilerParams(vmem_limit_bytes=16 * 1024 * 1024),
        cost_estimate=pl.CostEstimate(flops=0, bytes_accessed=w.size * 2, transcendentals=0),
        name="load",
    )(*(pltpu.with_memory_space_constraint(a, pltpu.HBM) for a in (*arrays, indices)))


def layer_kernel(tick, src_row, rows, brs, nzb, own_slot, prev_slot, aliased, *refs):
    refs = list(refs)
    meta, main, across, inside, w, bias = refs[:6]
    del refs[:6]
    prev = None
    if prev_slot is not None:
        prev = refs.pop(0)
    if aliased:
        refs.pop(0)
    emitted = refs.pop(0) if prev_slot is not None or own_slot is not None else None
    outer = None
    if own_slot is None:
        out, outer, xbuf, sems = refs
    else:
        out, xbuf, sems = refs
    edge = HALO * BLK
    width = brs * BLK

    def write(src, slot, first, count, sem):
        where = (slice(None), pl.ds(first * BLK, count * BLK))
        slot_tick, row = slot
        return pltpu.make_async_copy(
            src.at[where], emitted.at[slot_tick, pl.ds(row, rows), pl.ds(first * BLK, count * BLK)], sem
        )

    pieces = 4
    own = []
    if own_slot is not None:
        own = [write(out, own_slot, n * brs // pieces, brs // pieces, sems.at[1 + n]) for n in range(pieces)]
    if prev is not None:
        before = write(prev, prev_slot, 0, brs, sems.at[0])
        before.start()
    live = meta[brs * nzb] >= tick
    odd = meta[brs * nzb + 1]

    @pl.when(live)
    def _():
        src = pl.ds(src_row, rows)
        xbuf[:, edge : edge + width] = main[src, :]
        xbuf[:, pl.ds(pl.multiple_of(odd * (edge + width), BLK), edge)] = across[src, :]
        xbuf[:, pl.ds(pl.multiple_of((1 - odd) * (edge + width), BLK), edge)] = inside[src, :]
        for i in range(brs):
            picked = jnp.concatenate(
                [xbuf[:, pl.ds(pl.multiple_of(meta[i * nzb + k], BLK), BLK)] for k in range(nzb)], axis=1
            )
            cols = pl.ds(i * BLK, BLK)
            summed = jnp.dot(picked, w[i], preferred_element_type=jnp.float32) + bias[:, cols]
            made = jnp.maximum(summed, 0.0).astype(jnp.bfloat16)
            out[:, cols] = made
            if own and (i + 1) % (brs // pieces) == 0:
                own[i // (brs // pieces)].start()
        if outer is not None:
            outer[...] = out[:, pl.ds(pl.multiple_of(odd * (width - edge), BLK), edge)]

    @pl.when(jnp.logical_not(live))
    def _():
        out[...] = jnp.zeros_like(out)
        if outer is not None:
            outer[...] = jnp.zeros_like(outer)
        for copy in own:
            copy.start()

    if prev is not None:
        before.wait()
    for copy in own:
        copy.wait()


def apply_layer(tick, src_row, row, rows, last, operands, prev, prev_slot, emitted, emitted_aval):
    meta, main, across, inside, w, bias = operands
    brs, depth = w.shape[:2]
    nzb = depth // BLK
    width = brs * BLK
    edge = HALO * BLK
    args = [
        pltpu.with_memory_space_constraint(meta, pltpu.SMEM),
        *(pltpu.with_memory_space_constraint(a, pltpu.VMEM) for a in (main, across, inside, w, bias)),
    ]
    specs = [SMEM] + [VMEM] * 5
    out_shape = []
    out_specs = []
    scratch = [
        pltpu.VMEM((rows, width + 2 * edge), jnp.bfloat16),
        pltpu.SemaphoreType.DMA((5,)),
    ]
    aliases = {}
    if prev is not None:
        args.append(pltpu.with_memory_space_constraint(prev, pltpu.VMEM))
        specs.append(VMEM)
    if emitted is not None:
        aliases = {len(args): 0}
        args.append(emitted)
        specs.append(ANY)
    if prev is not None or last:
        out_shape.append(emitted_aval)
        out_specs.append(ANY)
    if last:
        scratch.insert(0, pltpu.VMEM((rows, width), jnp.bfloat16))
    else:
        out_shape += [pltpu.VMEM((rows, cols), jnp.bfloat16) for cols in (width, edge)]
        out_specs += [VMEM] * 2
    body = functools.partial(
        layer_kernel, tick, src_row, rows, brs, nzb, (tick, row) if last else None, prev_slot, emitted is not None
    )
    return pl.pallas_call(
        body,
        out_shape=tuple(out_shape),
        in_specs=specs,
        out_specs=tuple(out_specs),
        scratch_shapes=scratch,
        input_output_aliases=aliases,
        compiler_params=pltpu.CompilerParams(vmem_limit_bytes=8 * 1024 * 1024),
        cost_estimate=pl.CostEstimate(
            flops=18 * rows * brs * nzb * BLK * BLK, bytes_accessed=18 * w.size, transcendentals=0
        ),
        name=f"layer_t{tick}_r{row}",
    )(*args)


def edge_kernel(meta, main, far, after, edge):
    del far, after
    odd = meta[meta.shape[0] - 1]
    width = main.shape[1]
    edge[...] = main[:, pl.ds(pl.multiple_of((1 - odd) * (width - HALO * BLK), BLK), HALO * BLK)]


def inner_edge(meta, main, far, after):
    return pl.pallas_call(
        edge_kernel,
        out_shape=pltpu.VMEM((main.shape[0], HALO * BLK), main.dtype),
        in_specs=[SMEM, VMEM, ANY, ANY],
        out_specs=VMEM,
        compiler_params=pltpu.CompilerParams(vmem_limit_bytes=1024 * 1024),
        name="edge",
    )(
        pltpu.with_memory_space_constraint(meta, pltpu.SMEM),
        pltpu.with_memory_space_constraint(main, pltpu.VMEM),
        far,
        after,
    )


def shards(sections, blks, pending_groups, coefficient_tiles, source_block_indices, additive_offsets):
    block_rows, nzb = coefficient_tiles.shape[1:3]
    height, width = pending_groups.shape
    rows = height // CHUNKS
    edge = HALO * BLK
    emitted_aval = jax.ShapeDtypeStruct((TICKS, height, width), jnp.bfloat16)

    def hop(values, step, place, closed=True):
        pairs = [
            (s * blks + i, (s + step) % sections * blks + place(i) % blks)
            for s in range(sections if closed else sections - step)
            for i in range(blks)
        ]
        return lax.ppermute(values, ("section", "blk"), pairs)

    def across(i):
        return i + 1 if i % 2 else i - 1

    def inside(i):
        return i - 1 if i % 2 else i + 1

    odd = lax.axis_index("blk") % 2
    outer = lax.dynamic_slice_in_dim(pending_groups, odd * (width - edge), edge, axis=1)
    inner = lax.dynamic_slice_in_dim(pending_groups, (1 - odd) * (width - edge), edge, axis=1)
    far, near = hop(outer, 0, across), hop(inner, 0, inside)
    state, w, bias, meta = load(
        blks,
        pending_groups,
        coefficient_tiles.reshape(block_rows, nzb * BLK, BLK),
        additive_offsets,
        source_block_indices[0].T,
    )
    parts = [(state, far)] * CHUNKS
    emitted = prev = prev_slot = made = None
    for tick in range(TICKS):
        last = tick + 1 == TICKS
        for c in range(CHUNKS):
            main, far = parts[c]
            src_row = c * rows
            if tick > 0:
                near = hop(inner_edge(meta, main, far, made), 0, inside)
                src_row = 0
            outs = list(
                apply_layer(
                    tick, src_row, c * rows, rows, last, (meta, main, far, near, w, bias), prev, prev_slot, emitted, emitted_aval
                )
            )
            if prev is not None or last:
                emitted = outs.pop(0)
            prev = prev_slot = None
            if not last:
                prev, outer = outs
                made = prev
                prev_slot = (tick, c * rows)
                parts[c] = (hop(prev, 1, lambda i: i), hop(outer, 1, across, closed=False))
    return emitted


def solution(mesh):
    in_specs = (
        P("section", "blk"),
        P("section", "blk", None, None, None),
        P("section", "blk", None),
        P("section", "blk"),
    )
    out_specs = P(None, "section", "blk")
    body = functools.partial(shards, mesh.shape["section"], mesh.shape["blk"])
    return jax.shard_map(body, mesh=mesh, in_specs=in_specs, out_specs=out_specs, check_vma=False)
```

```python
import functools

import jax
import jax.numpy as jnp
from jax import lax
from jax.experimental import pallas as pl
from jax.experimental.pallas import tpu as pltpu
from jax.sharding import PartitionSpec as P

BLK = 128
HALO = 4
TICKS = 8
CHUNKS = 2
VMEM = pl.BlockSpec(memory_space=pltpu.VMEM)
SMEM = pl.BlockSpec(memory_space=pltpu.SMEM)
ANY = pl.BlockSpec(memory_space=pl.ANY)


def load_kernel(blks, state, w, bias, indices, state_out, w_out, bias_out, meta, raw, sems):
    copies = [
        pltpu.make_async_copy(src, dst, sems.at[i])
        for i, (src, dst) in enumerate(((indices, raw), (state, state_out), (bias, bias_out), (w, w_out)))
    ]
    for copy in copies:
        copy.start()
    nzb, brs = indices.shape
    columns = brs * blks
    start = lax.axis_index("blk") * brs - HALO
    meta[brs * nzb] = lax.axis_index("section")
    copies[0].wait()

    @pl.loop(0, brs)
    def _(i):
        for k in range(nzb):
            col = raw[k, i] - start
            col = jnp.where(col < 0, col + columns, col)
            meta[i * nzb + k] = jnp.where(col >= columns, col - columns, col) * BLK

    for copy in copies[1:]:
        copy.wait()


def load(blks, state, w, bias, indices):
    arrays = (state, w, bias)
    return pl.pallas_call(
        functools.partial(load_kernel, blks),
        out_shape=(
            *(pltpu.VMEM(a.shape, a.dtype) for a in arrays),
            pltpu.SMEM((indices.size + 1,), jnp.int32),
        ),
        in_specs=[ANY] * 4,
        out_specs=(VMEM,) * 3 + (SMEM,),
        scratch_shapes=[pltpu.SMEM(indices.shape, jnp.int32), pltpu.SemaphoreType.DMA((4,))],
        compiler_params=pltpu.CompilerParams(vmem_limit_bytes=16 * 1024 * 1024),
        cost_estimate=pl.CostEstimate(flops=0, bytes_accessed=w.size * 2, transcendentals=0),
        name="load",
    )(*(pltpu.with_memory_space_constraint(a, pltpu.HBM) for a in (*arrays, indices)))


def layer_kernel(tick, src_row, rows, brs, nzb, own_slot, prev_slot, aliased, *refs):
    refs = list(refs)
    meta, main, low, high, w, bias = refs[:6]
    del refs[:6]
    prev = refs.pop(0) if prev_slot is not None else None
    if aliased:
        refs.pop(0)
    emitted = refs.pop(0) if prev_slot is not None or own_slot is not None else None
    left = right = None
    if own_slot is None:
        out, left, right, xbuf, sems = refs
    else:
        out, xbuf, sems = refs
    edge = HALO * BLK
    width = brs * BLK

    def write(src, slot, first, count, sem):
        where = (slice(None), pl.ds(first * BLK, count * BLK))
        slot_tick, row = slot
        return pltpu.make_async_copy(
            src.at[where], emitted.at[slot_tick, pl.ds(row, rows), pl.ds(first * BLK, count * BLK)], sem
        )

    pieces = 4
    own = []
    if own_slot is not None:
        own = [write(out, own_slot, n * brs // pieces, brs // pieces, sems.at[1 + n]) for n in range(pieces)]
    if prev is not None:
        before = write(prev, prev_slot, 0, brs, sems.at[0])
        before.start()
    live = meta[brs * nzb] >= tick

    @pl.when(live)
    def _():
        src = pl.ds(src_row, rows)
        xbuf[:, 0:edge] = low[src, :]
        xbuf[:, edge : edge + width] = main[src, :]
        xbuf[:, edge + width : edge + width + edge] = high[src, :]
        for i in range(brs):
            picked = jnp.concatenate(
                [xbuf[:, pl.ds(pl.multiple_of(meta[i * nzb + k], BLK), BLK)] for k in range(nzb)], axis=1
            )
            cols = pl.ds(i * BLK, BLK)
            summed = jnp.dot(picked, w[i], preferred_element_type=jnp.float32) + bias[:, cols]
            made = jnp.maximum(summed, 0.0).astype(jnp.bfloat16)
            out[:, cols] = made
            if left is not None and i < HALO:
                left[:, cols] = made
            if right is not None and i >= brs - HALO:
                right[:, pl.ds((i - brs + HALO) * BLK, BLK)] = made
            if own and (i + 1) % (brs // pieces) == 0:
                own[i // (brs // pieces)].start()

    @pl.when(jnp.logical_not(live))
    def _():
        out[...] = jnp.zeros_like(out)
        if left is not None:
            left[...] = jnp.zeros_like(left)
            right[...] = jnp.zeros_like(right)
        for copy in own:
            copy.start()

    if prev is not None:
        before.wait()
    for copy in own:
        copy.wait()


def apply_layer(tick, src_row, row, rows, last, operands, prev, prev_slot, emitted, emitted_aval):
    meta, main, low, high, w, bias = operands
    brs, depth = w.shape[:2]
    nzb = depth // BLK
    width = brs * BLK
    edge = HALO * BLK
    args = [
        pltpu.with_memory_space_constraint(meta, pltpu.SMEM),
        *(pltpu.with_memory_space_constraint(a, pltpu.VMEM) for a in (main, low, high, w, bias)),
    ]
    specs = [SMEM] + [VMEM] * 5
    out_shape = []
    out_specs = []
    scratch = [
        pltpu.VMEM((rows, width + 2 * edge), jnp.bfloat16),
        pltpu.SemaphoreType.DMA((5,)),
    ]
    aliases = {}
    if prev is not None:
        args.append(pltpu.with_memory_space_constraint(prev, pltpu.VMEM))
        specs.append(VMEM)
    if emitted is not None:
        aliases = {len(args): 0}
        args.append(emitted)
        specs.append(ANY)
    if prev is not None or last:
        out_shape.append(emitted_aval)
        out_specs.append(ANY)
    if last:
        scratch.insert(0, pltpu.VMEM((rows, width), jnp.bfloat16))
    else:
        out_shape += [pltpu.VMEM((rows, cols), jnp.bfloat16) for cols in (width, edge, edge)]
        out_specs += [VMEM] * 3
    body = functools.partial(
        layer_kernel, tick, src_row, rows, brs, nzb, (tick, row) if last else None, prev_slot, emitted is not None
    )
    return pl.pallas_call(
        body,
        out_shape=tuple(out_shape),
        in_specs=specs,
        out_specs=tuple(out_specs),
        scratch_shapes=scratch,
        input_output_aliases=aliases,
        compiler_params=pltpu.CompilerParams(vmem_limit_bytes=8 * 1024 * 1024),
        cost_estimate=pl.CostEstimate(
            flops=20 * rows * brs * nzb * BLK * BLK, bytes_accessed=20 * w.size, transcendentals=0
        ),
        name=f"layer_t{tick}_r{row}",
    )(*args)


def shards(sections, blks, pending_groups, coefficient_tiles, source_block_indices, additive_offsets):
    block_rows, nzb = coefficient_tiles.shape[1:3]
    height, width = pending_groups.shape
    rows = height // CHUNKS
    edge = HALO * BLK
    emitted_aval = jax.ShapeDtypeStruct((TICKS, height, width), jnp.bfloat16)

    def hop(values, step, shift):
        pairs = [
            (s * blks + i, (s + step) % sections * blks + (i + shift) % blks)
            for s in range(sections)
            for i in range(blks)
        ]
        return lax.ppermute(values, ("section", "blk"), pairs)

    low = hop(pending_groups[:, width - edge :], 0, 1)
    high = hop(pending_groups[:, :edge], 0, -1)
    state, w, bias, meta = load(
        blks,
        pending_groups,
        coefficient_tiles.reshape(block_rows, nzb * BLK, BLK),
        additive_offsets,
        source_block_indices[0].T,
    )
    parts = [(state, low, high, c * rows) for c in range(CHUNKS)]
    emitted = prev = prev_slot = None
    for tick in range(TICKS):
        last = tick + 1 == TICKS
        for c in range(CHUNKS):
            main, low, high, src_row = parts[c]
            outs = list(
                apply_layer(
                    tick, src_row, c * rows, rows, last, (meta, main, low, high, w, bias), prev, prev_slot, emitted, emitted_aval
                )
            )
            if prev is not None or last:
                emitted = outs.pop(0)
            prev = prev_slot = None
            if not last:
                prev, left, right = outs
                prev_slot = (tick, c * rows)
                parts[c] = (hop(prev, 1, 0), hop(right, 1, 1), hop(left, 1, -1), 0)
    return emitted


def solution(mesh):
    in_specs = (
        P("section", "blk"),
        P("section", "blk", None, None, None),
        P("section", "blk", None),
        P("section", "blk"),
    )
    out_specs = P(None, "section", "blk")
    body = functools.partial(shards, mesh.shape["section"], mesh.shape["blk"])
    return jax.shard_map(body, mesh=mesh, in_specs=in_specs, out_specs=out_specs, check_vma=False)
```

```python
import functools

import jax
import jax.numpy as jnp
from jax import lax
from jax.experimental import pallas as pl
from jax.experimental.pallas import tpu as pltpu
from jax.sharding import PartitionSpec as P

BLK = 128
HALO = 4
TICKS = 8
CHUNKS = 2
VMEM = pl.BlockSpec(memory_space=pltpu.VMEM)
SMEM = pl.BlockSpec(memory_space=pltpu.SMEM)
ANY = pl.BlockSpec(memory_space=pl.ANY)


def load_kernel(blks, state, w, bias, indices, state_out, w_out, bias_out, meta, raw, sems):
    copies = [
        pltpu.make_async_copy(src, dst, sems.at[i])
        for i, (src, dst) in enumerate(((indices, raw), (state, state_out), (bias, bias_out), (w, w_out)))
    ]
    for copy in copies:
        copy.start()
    nzb, brs = indices.shape
    columns = brs * blks
    start = lax.axis_index("blk") * brs - HALO
    meta[brs * nzb] = lax.axis_index("section")
    copies[0].wait()

    @pl.loop(0, brs)
    def _(i):
        for k in range(nzb):
            col = raw[k, i] - start
            col = jnp.where(col < 0, col + columns, col)
            meta[i * nzb + k] = jnp.where(col >= columns, col - columns, col) * BLK

    for copy in copies[1:]:
        copy.wait()


def load(blks, state, w, bias, indices):
    arrays = (state, w, bias)
    return pl.pallas_call(
        functools.partial(load_kernel, blks),
        out_shape=(
            *(pltpu.VMEM(a.shape, a.dtype) for a in arrays),
            pltpu.SMEM((indices.size + 1,), jnp.int32),
        ),
        in_specs=[ANY] * 4,
        out_specs=(VMEM,) * 3 + (SMEM,),
        scratch_shapes=[pltpu.SMEM(indices.shape, jnp.int32), pltpu.SemaphoreType.DMA((4,))],
        compiler_params=pltpu.CompilerParams(vmem_limit_bytes=16 * 1024 * 1024),
        cost_estimate=pl.CostEstimate(flops=0, bytes_accessed=w.size * 2, transcendentals=0),
        name="load",
    )(*(pltpu.with_memory_space_constraint(a, pltpu.HBM) for a in (*arrays, indices)))


def layer_kernel(tick, src_row, rows, brs, nzb, own_slot, prev_slot, aliased, *refs):
    refs = list(refs)
    meta, main, low, high, w, bias = refs[:6]
    del refs[:6]
    prev = refs.pop(0) if prev_slot is not None else None
    if aliased:
        refs.pop(0)
    emitted = refs.pop(0) if prev_slot is not None or own_slot is not None else None
    left = right = None
    if own_slot is None:
        out, left, right, xbuf, sems = refs
    else:
        out, xbuf, sems = refs
    edge = HALO * BLK
    width = brs * BLK

    def write(src, slot, first, count, sem):
        where = (slice(None), pl.ds(first * BLK, count * BLK))
        slot_tick, row = slot
        return pltpu.make_async_copy(
            src.at[where], emitted.at[slot_tick, pl.ds(row, rows), pl.ds(first * BLK, count * BLK)], sem
        )

    pieces = 4
    own = []
    if own_slot is not None:
        own = [write(out, own_slot, n * brs // pieces, brs // pieces, sems.at[1 + n]) for n in range(pieces)]
    if prev is not None:
        before = write(prev, prev_slot, 0, brs, sems.at[0])
        before.start()
    live = meta[brs * nzb] >= tick

    @pl.when(live)
    def _():
        src = pl.ds(src_row, rows)
        xbuf[:, 0:edge] = low[src, :]
        xbuf[:, edge : edge + width] = main[src, :]
        xbuf[:, edge + width : edge + width + edge] = high[src, :]
        for i in range(brs):
            picked = jnp.concatenate(
                [xbuf[:, pl.ds(pl.multiple_of(meta[i * nzb + k], BLK), BLK)] for k in range(nzb)], axis=1
            )
            cols = pl.ds(i * BLK, BLK)
            summed = jnp.dot(picked, w[i], preferred_element_type=jnp.float32) + bias[:, cols]
            made = jnp.maximum(summed, 0.0).astype(jnp.bfloat16)
            out[:, cols] = made
            if left is not None and i < HALO:
                left[:, cols] = made
            if right is not None and i >= brs - HALO:
                right[:, pl.ds((i - brs + HALO) * BLK, BLK)] = made
            if own and (i + 1) % (brs // pieces) == 0:
                own[i // (brs // pieces)].start()

    @pl.when(jnp.logical_not(live))
    def _():
        out[...] = jnp.zeros_like(out)
        if left is not None:
            left[...] = jnp.zeros_like(left)
            right[...] = jnp.zeros_like(right)
        for copy in own:
            copy.start()

    if prev is not None:
        before.wait()
    for copy in own:
        copy.wait()


def apply_layer(tick, src_row, row, rows, last, operands, prev, prev_slot, emitted, emitted_aval):
    meta, main, low, high, w, bias = operands
    brs, depth = w.shape[:2]
    nzb = depth // BLK
    width = brs * BLK
    edge = HALO * BLK
    args = [
        pltpu.with_memory_space_constraint(meta, pltpu.SMEM),
        *(pltpu.with_memory_space_constraint(a, pltpu.VMEM) for a in (main, low, high, w, bias)),
    ]
    specs = [SMEM] + [VMEM] * 5
    out_shape = []
    out_specs = []
    scratch = [
        pltpu.VMEM((rows, width + 2 * edge), jnp.bfloat16),
        pltpu.SemaphoreType.DMA((5,)),
    ]
    aliases = {}
    if prev is not None:
        args.append(pltpu.with_memory_space_constraint(prev, pltpu.VMEM))
        specs.append(VMEM)
    if emitted is not None:
        aliases = {len(args): 0}
        args.append(emitted)
        specs.append(ANY)
    if prev is not None or last:
        out_shape.append(emitted_aval)
        out_specs.append(ANY)
    if last:
        scratch.insert(0, pltpu.VMEM((rows, width), jnp.bfloat16))
    else:
        out_shape += [pltpu.VMEM((rows, cols), jnp.bfloat16) for cols in (width, edge, edge)]
        out_specs += [VMEM] * 3
    body = functools.partial(
        layer_kernel, tick, src_row, rows, brs, nzb, (tick, row) if last else None, prev_slot, emitted is not None
    )
    return pl.pallas_call(
        body,
        out_shape=tuple(out_shape),
        in_specs=specs,
        out_specs=tuple(out_specs),
        scratch_shapes=scratch,
        input_output_aliases=aliases,
        compiler_params=pltpu.CompilerParams(vmem_limit_bytes=8 * 1024 * 1024),
        cost_estimate=pl.CostEstimate(
            flops=20 * rows * brs * nzb * BLK * BLK, bytes_accessed=20 * w.size, transcendentals=0
        ),
        name=f"layer_t{tick}_r{row}",
    )(*args)


def shards(sections, blks, pending_groups, coefficient_tiles, source_block_indices, additive_offsets):
    block_rows, nzb = coefficient_tiles.shape[1:3]
    height, width = pending_groups.shape
    rows = height // CHUNKS
    edge = HALO * BLK
    emitted_aval = jax.ShapeDtypeStruct((TICKS, height, width), jnp.bfloat16)

    def hop(values, step, shift, closed=True):
        pairs = [
            (s * blks + i, (s + step) % sections * blks + (i + shift) % blks)
            for s in range(sections if closed else sections - step)
            for i in range(blks)
        ]
        return lax.ppermute(values, ("section", "blk"), pairs)

    low = hop(pending_groups[:, width - edge :], 0, 1)
    high = hop(pending_groups[:, :edge], 0, -1)
    state, w, bias, meta = load(
        blks,
        pending_groups,
        coefficient_tiles.reshape(block_rows, nzb * BLK, BLK),
        additive_offsets,
        source_block_indices[0].T,
    )
    parts = [(state, low, high, c * rows) for c in range(CHUNKS)]
    emitted = prev = prev_slot = None
    for tick in range(TICKS):
        last = tick + 1 == TICKS
        for c in range(CHUNKS):
            main, low, high, src_row = parts[c]
            outs = list(
                apply_layer(
                    tick, src_row, c * rows, rows, last, (meta, main, low, high, w, bias), prev, prev_slot, emitted, emitted_aval
                )
            )
            if prev is not None or last:
                emitted = outs.pop(0)
            prev = prev_slot = None
            if not last:
                prev, left, right = outs
                prev_slot = (tick, c * rows)
                parts[c] = (hop(prev, 1, 0), hop(right, 1, 1), hop(left, 1, -1, closed=False), 0)
    return emitted


def solution(mesh):
    in_specs = (
        P("section", "blk"),
        P("section", "blk", None, None, None),
        P("section", "blk", None),
        P("section", "blk"),
    )
    out_specs = P(None, "section", "blk")
    body = functools.partial(shards, mesh.shape["section"], mesh.shape["blk"])
    return jax.shard_map(body, mesh=mesh, in_specs=in_specs, out_specs=out_specs, check_vma=False)
```

```python
import functools

import jax
import jax.numpy as jnp
from jax import lax
from jax.experimental import pallas as pl
from jax.experimental.pallas import tpu as pltpu
from jax.sharding import PartitionSpec as P

BLK = 128
HALO = 4
TICKS = 8
CHUNKS = 2
PIECES = 8
VMEM = pl.BlockSpec(memory_space=pltpu.VMEM)
SMEM = pl.BlockSpec(memory_space=pltpu.SMEM)
ANY = pl.BlockSpec(memory_space=pl.ANY)


def load_kernel(blks, state, w, bias, indices, state_out, w_out, bias_out, meta, raw, sems):
    part = w.shape[0] // PIECES
    copies = [
        pltpu.make_async_copy(src, dst, sems.at[i])
        for i, (src, dst) in enumerate(
            [(indices, raw), (state, state_out), (bias, bias_out)]
            + [(w.at[pl.ds(n * part, part)], w_out.at[pl.ds(n * part, part)]) for n in range(PIECES)]
        )
    ]
    for copy in copies:
        copy.start()
    nzb, brs = indices.shape
    columns = brs * blks
    start = lax.axis_index("blk") * brs - HALO
    meta[brs * nzb] = lax.axis_index("section")
    copies[0].wait()

    @pl.loop(0, brs)
    def _(i):
        for k in range(nzb):
            col = raw[k, i] - start
            col = jnp.where(col < 0, col + columns, col)
            meta[i * nzb + k] = jnp.where(col >= columns, col - columns, col) * BLK

    for copy in copies[1:]:
        copy.wait()


def load(blks, state, w, bias, indices):
    arrays = (state, w, bias)
    return pl.pallas_call(
        functools.partial(load_kernel, blks),
        out_shape=(
            *(pltpu.VMEM(a.shape, a.dtype) for a in arrays),
            pltpu.SMEM((indices.size + 1,), jnp.int32),
        ),
        in_specs=[ANY] * 4,
        out_specs=(VMEM,) * 3 + (SMEM,),
        scratch_shapes=[pltpu.SMEM(indices.shape, jnp.int32), pltpu.SemaphoreType.DMA((3 + PIECES,))],
        compiler_params=pltpu.CompilerParams(vmem_limit_bytes=16 * 1024 * 1024),
        cost_estimate=pl.CostEstimate(flops=0, bytes_accessed=w.size * 2, transcendentals=0),
        name="load",
    )(*(pltpu.with_memory_space_constraint(a, pltpu.HBM) for a in (*arrays, indices)))


def layer_kernel(tick, src_row, rows, brs, nzb, own_slot, prev_slot, aliased, *refs):
    refs = list(refs)
    meta, main, low, high, w, bias = refs[:6]
    del refs[:6]
    prev = refs.pop(0) if prev_slot is not None else None
    if aliased:
        refs.pop(0)
    emitted = refs.pop(0) if prev_slot is not None or own_slot is not None else None
    left = right = None
    if own_slot is None:
        out, left, right, xbuf, sems = refs
    else:
        out, xbuf, sems = refs
    edge = HALO * BLK
    width = brs * BLK

    def write(src, slot, first, count, sem):
        where = (slice(None), pl.ds(first * BLK, count * BLK))
        slot_tick, row = slot
        return pltpu.make_async_copy(
            src.at[where], emitted.at[slot_tick, pl.ds(row, rows), pl.ds(first * BLK, count * BLK)], sem
        )

    pieces = 4
    own = []
    if own_slot is not None:
        own = [write(out, own_slot, n * brs // pieces, brs // pieces, sems.at[1 + n]) for n in range(pieces)]
    if prev is not None:
        before = write(prev, prev_slot, 0, brs, sems.at[0])
        before.start()
    live = meta[brs * nzb] >= tick

    @pl.when(live)
    def _():
        src = pl.ds(src_row, rows)
        xbuf[:, 0:edge] = low[src, :]
        xbuf[:, edge : edge + width] = main[src, :]
        xbuf[:, edge + width : edge + width + edge] = high[src, :]
        for i in range(brs):
            picked = jnp.concatenate(
                [xbuf[:, pl.ds(pl.multiple_of(meta[i * nzb + k], BLK), BLK)] for k in range(nzb)], axis=1
            )
            cols = pl.ds(i * BLK, BLK)
            summed = jnp.dot(picked, w[i], preferred_element_type=jnp.float32) + bias[:, cols]
            made = jnp.maximum(summed, 0.0).astype(jnp.bfloat16)
            out[:, cols] = made
            if left is not None and i < HALO:
                left[:, cols] = made
            if right is not None and i >= brs - HALO:
                right[:, pl.ds((i - brs + HALO) * BLK, BLK)] = made
            if own and (i + 1) % (brs // pieces) == 0:
                own[i // (brs // pieces)].start()

    @pl.when(jnp.logical_not(live))
    def _():
        out[...] = jnp.zeros_like(out)
        if left is not None:
            left[...] = jnp.zeros_like(left)
            right[...] = jnp.zeros_like(right)
        for copy in own:
            copy.start()

    if prev is not None:
        before.wait()
    for copy in own:
        copy.wait()


def apply_layer(tick, src_row, row, rows, last, operands, prev, prev_slot, emitted, emitted_aval):
    meta, main, low, high, w, bias = operands
    brs, depth = w.shape[:2]
    nzb = depth // BLK
    width = brs * BLK
    edge = HALO * BLK
    args = [
        pltpu.with_memory_space_constraint(meta, pltpu.SMEM),
        *(pltpu.with_memory_space_constraint(a, pltpu.VMEM) for a in (main, low, high, w, bias)),
    ]
    specs = [SMEM] + [VMEM] * 5
    out_shape = []
    out_specs = []
    scratch = [
        pltpu.VMEM((rows, width + 2 * edge), jnp.bfloat16),
        pltpu.SemaphoreType.DMA((5,)),
    ]
    aliases = {}
    if prev is not None:
        args.append(pltpu.with_memory_space_constraint(prev, pltpu.VMEM))
        specs.append(VMEM)
    if emitted is not None:
        aliases = {len(args): 0}
        args.append(emitted)
        specs.append(ANY)
    if prev is not None or last:
        out_shape.append(emitted_aval)
        out_specs.append(ANY)
    if last:
        scratch.insert(0, pltpu.VMEM((rows, width), jnp.bfloat16))
    else:
        out_shape += [pltpu.VMEM((rows, cols), jnp.bfloat16) for cols in (width, edge, edge)]
        out_specs += [VMEM] * 3
    body = functools.partial(
        layer_kernel, tick, src_row, rows, brs, nzb, (tick, row) if last else None, prev_slot, emitted is not None
    )
    return pl.pallas_call(
        body,
        out_shape=tuple(out_shape),
        in_specs=specs,
        out_specs=tuple(out_specs),
        scratch_shapes=scratch,
        input_output_aliases=aliases,
        compiler_params=pltpu.CompilerParams(vmem_limit_bytes=8 * 1024 * 1024),
        cost_estimate=pl.CostEstimate(
            flops=20 * rows * brs * nzb * BLK * BLK, bytes_accessed=20 * w.size, transcendentals=0
        ),
        name=f"layer_t{tick}_r{row}",
    )(*args)


def shards(sections, blks, pending_groups, coefficient_tiles, source_block_indices, additive_offsets):
    block_rows, nzb = coefficient_tiles.shape[1:3]
    height, width = pending_groups.shape
    rows = height // CHUNKS
    edge = HALO * BLK
    emitted_aval = jax.ShapeDtypeStruct((TICKS, height, width), jnp.bfloat16)

    def hop(values, step, shift):
        pairs = [
            (s * blks + i, (s + step) % sections * blks + (i + shift) % blks)
            for s in range(sections)
            for i in range(blks)
        ]
        return lax.ppermute(values, ("section", "blk"), pairs)

    low = hop(pending_groups[:, width - edge :], 0, 1)
    high = hop(pending_groups[:, :edge], 0, -1)
    state, w, bias, meta = load(
        blks,
        pending_groups,
        coefficient_tiles.reshape(block_rows, nzb * BLK, BLK),
        additive_offsets,
        source_block_indices[0].T,
    )
    parts = [(state, low, high, c * rows) for c in range(CHUNKS)]
    emitted = prev = prev_slot = None
    for tick in range(TICKS):
        last = tick + 1 == TICKS
        for c in range(CHUNKS):
            main, low, high, src_row = parts[c]
            outs = list(
                apply_layer(
                    tick, src_row, c * rows, rows, last, (meta, main, low, high, w, bias), prev, prev_slot, emitted, emitted_aval
                )
            )
            if prev is not None or last:
                emitted = outs.pop(0)
            prev = prev_slot = None
            if not last:
                prev, left, right = outs
                prev_slot = (tick, c * rows)
                parts[c] = (hop(prev, 1, 0), hop(right, 1, 1), hop(left, 1, -1), 0)
    return emitted


def solution(mesh):
    in_specs = (
        P("section", "blk"),
        P("section", "blk", None, None, None),
        P("section", "blk", None),
        P("section", "blk"),
    )
    out_specs = P(None, "section", "blk")
    body = functools.partial(shards, mesh.shape["section"], mesh.shape["blk"])
    return jax.shard_map(body, mesh=mesh, in_specs=in_specs, out_specs=out_specs, check_vma=False)
```
